512 devices in a mesh: team: 64 (over z_hi, y, core), loop: 8 (over z_lo, x).
Axes of the slice: x: 4, y: 8, z: 8 (z_hi: 4, z_lo: 2; z = z_hi * 2 + z_lo), core: 2. Of those that a mesh axis runs over, the one named last changes fastest.
Arguments:
- src_pos: float32 [3, 262144], P(None, ('team', 'loop')), may hold values from -6 to 6
- src_vel: float32 [3, 262144], P(None, ('team', 'loop')), may hold values from -5 to 5
- src_mass: float32 [262144], P(('team', 'loop')), may hold values from 0.2 to 5
- old_accel: float32 [6, 8192], P(None, ('team', 'loop')), may hold values from -6 to 6
- active_index: int32 [8192], P(('team', 'loop')), may hold values from 0 to 511, as said below
- active_level: int32 [8192], P(('team', 'loop')), may hold values from 0 to 3
- tile_id: int32 [8192], P(('team', 'loop')), may hold values from 0 to 511
- tile_offset: int32 [2, 8192], P(None, ('team', 'loop')), may hold values from 16 to 112
Outputs:
- new_state: float32 [12, 8192], P(None, ('team', 'loop'))
- image: float32 [2, 512, 128, 128], P(None, ('team', 'loop'))
The draws below stay inside these ranges and needn't reach their ends.
Inputs may be any that keep to these rules, and one draw needn't show every extreme that they name: `active_index`: the 16 entries of one device are distinct rows of that device's 512 source stars.
All inputs are finite; a program needn't handle non-finite values.
Results may differ from the reference program's by a relative error of at most 0.0027.
Values sent between devices are 32-bit elements; how exact they have to be, the bound alone decides.
A program may use at most 64 MiB of HBM per device.

```python
import math
import jax
import jax.numpy as jnp
import numpy as np
from jax import lax

SRC_DEV = 512
ACT_DEV = 16
TILE_W = 128
LEVELS = 4
NSRC = 262144
ACTIVE = 8192
TILES = 512


def draw_active_index(key, part):
    block_count = ACTIVE // ACT_DEV

    def per_block(block_key):
        key_a, key_b = jax.random.split(block_key)
        inner = jax.random.permutation(key_a, SRC_DEV - 2)[:ACT_DEV - 2] + 1
        picked = jnp.concatenate([jnp.array([0, SRC_DEV - 1], jnp.int32), inner.astype(jnp.int32)])
        return picked[jax.random.permutation(key_b, ACT_DEV)]
    return jax.vmap(per_block)(jax.random.split(key, block_count)).reshape(ACTIVE).astype(jnp.int32)


def draw_active_level(key, part):
    key_a, key_b = jax.random.split(jax.random.fold_in(key, 7))
    levels = jax.random.randint(key_a, (ACTIVE,), 0, LEVELS)
    spot_at = jax.random.randint(key_b, (), 0, ACTIVE - 1)
    levels = levels.at[spot_at].set(0).at[spot_at + 1].set(LEVELS - 1)
    return levels.astype(jnp.int32)


def with_ends(result, key, low, high):
    longest = result.shape.index(max(result.shape))
    spots = []
    for shift in (0, 1):
        where = [jax.random.randint(jax.random.fold_in(key, axis), (), 0, length) for axis, length in enumerate(result.shape)]
        where[longest] = (where[longest] + shift) % result.shape[longest]
        spots.append(tuple(where))
    return result.at[spots[0]].set(low).at[spots[1]].set(high)


def level_of(own_key, shape, cuts, smallest, largest):
    gain = 1.0
    for axis_at, shards_of in cuts:
        draws = jax.random.uniform(jax.random.fold_in(jax.random.fold_in(own_key, 6), axis_at), (shards_of,), jnp.float32, smallest / len(cuts), largest / len(cuts))
        gain = gain * jnp.repeat(jnp.exp(draws), shape[axis_at] // shards_of).reshape((-1,) + (1,) * (len(shape) - 1 - axis_at))
    return gain


def cumulative_ranks(number_of, slope):
    weights = [(1 << 20) // math.isqrt(standing ** slope) + 1 for standing in range(1, number_of + 1)]
    scale = 1 + sum(weights) // (1 << 30)
    return np.cumsum(np.array([max(1, weight // scale) for weight in weights]))


def ranked(own_key, extent, amount, slope):
    listing = cumulative_ranks(amount, slope)
    pick = jax.random.randint(jax.random.fold_in(own_key, 1), extent, 0, int(listing[amount - 1]))
    standing = jnp.searchsorted(jnp.asarray(listing, jnp.int32), pick, side="right")
    return jax.random.permutation(jax.random.fold_in(own_key, 2), amount)[standing].astype(jnp.int32)


def centred(rng, shape, spread, limit, cuts=(), held_as=jnp.bfloat16):
    loudness = level_of(rng, shape, cuts, -0.22, 0.18) if cuts else 1.0
    entries = jax.random.normal(rng, shape, jnp.float32) * spread * loudness
    return jnp.minimum(jnp.maximum(entries, -limit), limit).astype(held_as)


def setup_inputs(seed: int = 0) -> dict:
    key_of = jax.random.split(jax.random.key(seed), 9)
    src_pos = centred(key_of[0], (3, NSRC), 1.0, 6.0, ((1, 512),), jnp.float32)
    src_vel = centred(key_of[1], (3, NSRC), 0.7, 5.0, ((1, 512),), jnp.float32)
    src_mass = jnp.clip(jnp.exp(math.log(5.0) - 3.218876 * jax.random.uniform(key_of[2], (NSRC,), jnp.float32) ** level_of(key_of[2], (NSRC,), ((0, 512),), -0.2, 0.2)), 0.2, 5.0)
    old_accel = centred(key_of[3], (6, ACTIVE), 1.0, 6.0, ((1, 512),), jnp.float32)
    active_index = draw_active_index(jax.random.fold_in(key_of[8], 71), 0)
    active_level = draw_active_level(jax.random.fold_in(key_of[8], 71), 0)
    tile_id = with_ends(ranked(key_of[6], (ACTIVE,), TILES, 2), jax.random.fold_in(key_of[6], 3), 0, TILES - 1).astype(jnp.int32)
    tile_offset = with_ends(jax.random.randint(key_of[7], (2, ACTIVE), TILE_W // 8, TILE_W - TILE_W // 8 + 1), jax.random.fold_in(key_of[7], 1), TILE_W // 8, (TILE_W - TILE_W // 8 + 1) - 1).astype(jnp.int32)
    return {"src_pos": src_pos, "src_vel": src_vel, "src_mass": src_mass, "old_accel": old_accel, "active_index": active_index, "active_level": active_level, "tile_id": tile_id, "tile_offset": tile_offset}


def pair_terms(tgt_pos, tgt_vel, blk_pos, blk_vel, blk_mass, gravity, soften_sq):
    separation = blk_pos[:, None, :] - tgt_pos[:, :, None]
    rel_vel = blk_vel[:, None, :] - tgt_vel[:, :, None]
    dist_sq = lax.optimization_barrier(jnp.sum(separation * separation, axis=0)) + soften_sq
    inverse = lax.rsqrt(dist_sq)
    inverse_sq = inverse * inverse
    strength = (gravity * blk_mass)[None, :] * inverse * inverse_sq
    radial = 3.0 * lax.optimization_barrier(jnp.sum(separation * rel_vel, axis=0)) * inverse_sq
    acceleration = lax.optimization_barrier(jnp.sum(strength[None] * separation, axis=2))
    jerk_sum = lax.optimization_barrier(jnp.sum(strength[None] * (rel_vel - radial[None] * separation), axis=2))
    return jnp.concatenate([acceleration, jerk_sum], axis=0)

def correct(targets, force, old_accel, level_float):
    step_len = jnp.exp2(-level_float)
    accel_gap = old_accel[0:3] - force[0:3]
    first_term = -6.0 * accel_gap - step_len * (4.0 * old_accel[3:6] + 2.0 * force[3:6])
    second = 12.0 * accel_gap + 6.0 * step_len * (old_accel[3:6] + force[3:6])
    new_pos = targets[0:3] + step_len * step_len * (first_term / 24.0 + second / 120.0)
    new_vel = targets[3:6] + step_len * (first_term / 6.0 + second / 24.0)
    return jnp.concatenate([new_pos, new_vel, force], axis=0)

def ingredients(new_state, star_mass, offsets, width):
    swing_cells = width / 16.0
    centre_y = offsets[0] + swing_cells * jnp.tanh(new_state[1])
    centre_x = offsets[1] + swing_cells * jnp.tanh(new_state[0])
    return jnp.stack([star_mass, star_mass * new_state[5] * new_state[5], centre_y, centre_x])

def kernel_rows(centre, width):
    cell_mid = jnp.arange(width, dtype=jnp.float32) + 0.5
    scaled = (cell_mid[None, :] - centre[:, None]) / (width / 40.0)
    return jnp.exp(-0.5 * scaled * scaled)

def reference(src_pos, src_vel, src_mass, old_accel, active_index, active_level, tile_id, tile_offset):
    gravity = 1.0 / NSRC
    soften_sq = float(NSRC) ** (-2.0 / 3.0)
    owner = jnp.arange(ACTIVE, dtype=jnp.int32) // ACT_DEV
    source_row = (owner * SRC_DEV + active_index).astype(jnp.int32)
    targets = jnp.concatenate([jnp.take(src_pos, source_row, axis=1), jnp.take(src_vel, source_row, axis=1)], axis=0)
    star_mass = jnp.take(src_mass, source_row, axis=0)
    block_len = math.gcd(NSRC, 1024)

    def add_block(running, block_idx):
        start_row = (block_idx * block_len).astype(jnp.int32)
        blk_pos = lax.dynamic_slice_in_dim(src_pos, start_row, block_len, 1)
        blk_vel = lax.dynamic_slice_in_dim(src_vel, start_row, block_len, 1)
        blk_mass = lax.dynamic_slice_in_dim(src_mass, start_row, block_len, 0)
        return (running + pair_terms(targets[0:3], targets[3:6], blk_pos, blk_vel, blk_mass, gravity, soften_sq), None)
    force = lax.scan(add_block, jnp.zeros((6, ACTIVE), jnp.float32), jnp.arange(NSRC // block_len, dtype=jnp.int32))[0]
    new_state = correct(targets, force, old_accel, active_level.astype(jnp.float32))
    deposit_parts = ingredients(new_state, star_mass, tile_offset.astype(jnp.float32), TILE_W)
    left_rows = (deposit_parts[0:2, :, None] * kernel_rows(deposit_parts[2], TILE_W)[None]).astype(jnp.bfloat16)
    right_rows = kernel_rows(deposit_parts[3], TILE_W).astype(jnp.bfloat16)
    star_block = math.gcd(ACTIVE, 256)

    def add_stars(block_idx, image_sum):
        start_row = (block_idx * star_block).astype(jnp.int32)
        left_block = lax.dynamic_slice_in_dim(left_rows, start_row, star_block, 1).astype(jnp.float32)
        right_block = lax.dynamic_slice_in_dim(right_rows, start_row, star_block, 0).astype(jnp.float32)
        tile_block = lax.dynamic_slice_in_dim(tile_id, start_row, star_block, 0)
        outer_prod = left_block[:, :, :, None] * right_block[None, :, None, :]
        return image_sum.at[:, tile_block].add(outer_prod)
    image = lax.fori_loop(0, ACTIVE // star_block, add_stars, jnp.zeros((2, TILES, TILE_W, TILE_W), jnp.float32))
    return (new_state, image)
```

```python
import functools

import jax
import jax.numpy as jnp
from jax import lax
from jax.experimental import pallas as pl
from jax.experimental.pallas import tpu as pltpu
from jax.sharding import PartitionSpec as P

MESH = pl.DeviceIdType.MESH
F32, BF16 = jnp.float32, jnp.bfloat16
RING = 8
SRC = 512
ACT = 16
LANES = 128
TILE_W = 128
ROWS_B = 256


def split3(v):
    a = v.astype(BF16)
    r = v - a.astype(F32)
    b = r.astype(BF16)
    return a, b, (r - b.astype(F32)).astype(BF16)


def wide3(v):
    return [p.astype(F32) for p in split3(v)]


def wide2(v):
    a = v.astype(BF16).astype(F32)
    return a, (v - a).astype(BF16).astype(F32)


def coarse(v):
    return jnp.round(v * 32.0) * (1.0 / 32.0)


def pad_rows(v, rows):
    gap = jnp.zeros((rows - v.shape[0], v.shape[1]), v.dtype)
    return jnp.concatenate([v, gap], axis=0)


def features(pos, vel, soften):
    h, u = coarse(pos), coarse(vel)
    l, m = pos - h, vel - u
    l1, l2 = wide2(l)
    m1, m2 = wide2(m)
    total = lambda v: jnp.sum(v, axis=0, keepdims=True)
    hh = wide3(total(h * h))
    hl = wide3(total(2.0 * h * l + l * l) + (0.0 if soften is None else soften))
    hu = wide3(total(h * u))
    hm = wide3(total(h * m + l * u + l * m))
    ones = [jnp.ones_like(h)]
    if soften is None:
        near = [h] + hh + ones + [h, h, l1, l2, l1, l1, l2] + hl + ones
        dots = [h, u] + hu + ones + [h, h, m1, m2, l1, l2, u, u, l1, l1, l2, m1, m1, m2] + hm + ones
    else:
        near = [-2.0 * h] + ones + hh
        near += [-2.0 * l1, -2.0 * l2, -2.0 * h, -2.0 * h, -2.0 * l1, -2.0 * l2, -2.0 * l1] + ones + hl
        dots = [-u, -h] + ones + hu
        dots += [-m1, -m2, -h, -h, -u, -u, -l1, -l2, -m1, -m2, -m1, -l1, -l2, -l1] + ones + hm
    near = jnp.concatenate(near, axis=0)
    return near.shape[0], pad_rows(jnp.concatenate([near] + dots, axis=0), LANES)


def correct(targets, force, old_accel, level):
    step = jnp.exp2(-level)
    gap = old_accel[0:3] - force[0:3]
    first = -6.0 * gap - step * (4.0 * old_accel[3:6] + 2.0 * force[3:6])
    second = 12.0 * gap + 6.0 * step * (old_accel[3:6] + force[3:6])
    pos = targets[0:3] + step * step * (first / 24.0 + second / 120.0)
    vel = targets[3:6] + step * (first / 6.0 + second / 24.0)
    return jnp.concatenate([pos, vel, force], axis=0)


def kernel(
    gravity, soften,
    pos_ref, vel_ref, mass_ref, old_ref, index_ref, level_ref, tile_ref, offset_ref,
    state_ref, image_ref,
    source, small, own, own_in, block, targets, near_f, dots_f, weights, target_f, force_acc,
    part, part_in, half, half_in, spread, gathered, left, right,
    send_sem, recv_sem,
):
    team, loop = lax.axis_index("team"), lax.axis_index("loop")
    zh, y, c = team // 16, (team // 2) % 8, team % 2
    zl, x = loop // 4, loop % 4
    z, xc = zh * 2 + zl, x * 2 + c

    def at(y, z, xc):
        return ((z // 2) * 16 + y * 2 + xc % 2, (z % 2) * 4 + xc // 2)

    def y_peer(k):
        return at((y + k) % 8, z, xc)

    def z_peer(k):
        return at(y, (z + k) % 8, xc)

    def x_peer(k):
        return at(y, z, (xc + k) % 8)

    barrier = pltpu.get_barrier_semaphore()
    for k in range(1, RING):
        for peer in (y_peer(k), z_peer(k), x_peer(k)):
            pl.semaphore_signal(barrier, inc=1, device_id=peer, device_id_type=MESH)

    def copy(stage, k, src, dst, peer):
        return pltpu.make_async_remote_copy(
            src_ref=src,
            dst_ref=dst,
            send_sem=send_sem.at[stage, k],
            recv_sem=recv_sem.at[stage, k],
            device_id=peer,
            device_id_type=MESH,
        )

    source[0, 0:3, :] = pos_ref[...]
    source[0, 3:6, :] = vel_ref[...]
    source[0, 6:7, :] = mass_ref[...].reshape(1, SRC)
    source[0, 7:8, :] = jnp.zeros((1, SRC), F32)
    small[...] = jnp.zeros_like(small)
    small[0:6, 0:ACT] = old_ref[...]
    small[6:7, 0:ACT] = level_ref[...].reshape(1, ACT).astype(F32)
    small[7:8, 0:ACT] = tile_ref[...].reshape(1, ACT).astype(F32)
    small[8:10, 0:ACT] = offset_ref[...].astype(F32)
    small[10:11, 0:ACT] = index_ref[...].reshape(1, ACT).astype(F32)
    placed = pltpu.roll(small[...], y * ACT, 1)
    star = lax.broadcasted_iota(jnp.int32, (SRC, LANES), 0).astype(F32)
    lane = lax.broadcasted_iota(jnp.int32, (SRC, LANES), 1)
    chosen = jnp.where((star == placed[10:11]) & (lane // ACT == y), 1.0, 0.0).astype(BF16)
    pieces = jnp.concatenate(wide3(source[0]), axis=0).astype(BF16)
    picked = jnp.dot(pieces, chosen, preferred_element_type=F32)
    own[0:8, :] = picked[0:8] + picked[8:16] + picked[16:24]
    own[8:24, :] = placed

    pl.semaphore_wait(barrier, 3 * (RING - 1))

    to_y = [copy(0, k, own, own_in.at[k], y_peer(k)) for k in range(1, RING)]
    to_z = [copy(1, k, source.at[0], source.at[k], z_peer(k)) for k in range(1, RING)]
    for k in range(1, RING):
        to_y[k - 1].start()
    for k in range(1, RING):
        to_z[k - 1].start()

    def prepare_source(k):
        s = source[k]
        cut, f = features(s[0:3], s[3:6], None)
        row = lax.broadcasted_iota(jnp.int32, f.shape, 0)
        lanes = pl.ds(pl.multiple_of(k * SRC, SRC), SRC)
        near_f[:, lanes] = jnp.where(row < cut, f, 0.0).astype(BF16)
        dots_f[:, lanes] = jnp.where(row < cut, 0.0, f).astype(BF16)
        mass = s[6:7]
        moments = jnp.concatenate([s[0:3] * mass, s[3:6] * mass, mass, jnp.zeros_like(mass)], axis=0)
        moments = pad_rows(jnp.concatenate(wide3(moments), axis=0), LANES)
        columns = jnp.transpose(moments)
        weights[0, lanes, :] = columns.astype(BF16)
        weights[1, lanes, :] = pltpu.roll(columns, 32, 1).astype(BF16)

    prepare_source(0)

    full = own[...]
    for k in range(1, RING):
        to_y[k - 1].wait_recv()
        full = full + own_in[k]
    block[...] = full[8:24]
    targets[0] = full[0:8]

    to_x = [copy(2, k, targets.at[0], targets.at[k], x_peer(k)) for k in range(1, RING)]
    for k in range(1, RING):
        to_x[k - 1].start()

    for k in range(1, RING):
        to_z[k - 1].wait_recv()

    def prepare_step(k, carry):
        prepare_source(k)
        return carry

    lax.fori_loop(1, RING, prepare_step, 0)

    for k in range(1, RING):
        to_x[k - 1].wait_recv()

    def prepare_target(k, carry):
        t = targets[k]
        f = features(t[0:3], t[3:6], soften)[1]
        target_f[pl.ds(pl.multiple_of(k * LANES, LANES), LANES), :] = jnp.transpose(f).astype(BF16)
        return carry

    lax.fori_loop(0, RING, prepare_target, 0)

    def force_step(step, carry):
        rows = pl.ds(pl.multiple_of(step * ROWS_B, ROWS_B), ROWS_B)
        f = target_f[rows, :]
        dist_sq = jnp.dot(f, near_f[...], preferred_element_type=F32)
        dots = jnp.dot(f, dots_f[...], preferred_element_type=F32)
        inverse = lax.rsqrt(dist_sq)
        inverse_sq = inverse * inverse
        strength = inverse * inverse_sq
        radial = (strength * inverse_sq) * dots
        force_acc[rows, :] = jnp.dot(
            strength.astype(BF16), weights[0], preferred_element_type=F32
        ) + jnp.dot(radial.astype(BF16), weights[1], preferred_element_type=F32)
        return carry

    lax.fori_loop(0, RING * LANES // ROWS_B, force_step, 0)

    def combine_step(k, carry):
        sums = jnp.transpose(force_acc[pl.ds(pl.multiple_of(k * LANES, LANES), LANES), :])
        plain = sums[0:8] + sums[8:16] + sums[16:24]
        tilted = sums[32:40] + sums[40:48] + sums[48:56]
        t = targets[k]
        accel = plain[0:3] - t[0:3] * plain[6:7]
        jerk = (plain[3:6] - t[3:6] * plain[6:7]) - 3.0 * (tilted[0:3] - t[0:3] * tilted[6:7])
        part[k] = pad_rows(gravity * jnp.concatenate([accel, jerk], axis=0), 8)
        return carry

    lax.fori_loop(0, RING, combine_step, 0)

    back_x = [copy(3, k, part.at[k], part_in.at[k], x_peer(-k)) for k in range(1, RING)]
    for k in range(1, RING):
        back_x[k - 1].start()
    total = part[0]
    for k in range(1, RING):
        back_x[k - 1].wait_recv()
        total = total + part_in[k]
    half[...] = total
    around_y = [copy(4, k, half, half_in.at[k], y_peer(k)) for k in range(1, RING)]
    for k in range(1, RING):
        around_y[k - 1].start()
    for k in range(1, RING):
        around_y[k - 1].wait_recv()
        total = total + half_in[k]

    stars = targets[0]
    rest = block[...]
    state = correct(stars[0:6], total[0:6], rest[0:6], rest[6:7])
    centre_y = rest[8:9] + (TILE_W / 16.0) * jnp.tanh(state[1:2])
    centre_x = rest[9:10] + (TILE_W / 16.0) * jnp.tanh(state[0:1])
    mass = stars[6:7]
    spread[0] = pad_rows(
        jnp.concatenate([mass, mass * state[5:6] * state[5:6], centre_y, centre_x, rest[7:8]], axis=0), 8
    )
    deposit_z = [copy(5, k, spread.at[0], spread.at[k], z_peer(k)) for k in range(1, RING)]
    for k in range(1, RING):
        deposit_z[k - 1].start()
    shifted = pltpu.roll(pad_rows(state, 16), (LANES - y * ACT) % LANES, 1)
    state_ref[...] = shifted[0:12, 0:ACT]
    for k in range(1, RING):
        deposit_z[k - 1].wait_recv()
    deposit_x = [copy(6, k, spread, gathered.at[k], x_peer(k)) for k in range(1, RING)]
    for k in range(1, RING):
        deposit_x[k - 1].start()

    mine = (team * 8 + loop).astype(F32)
    cell = lax.broadcasted_iota(jnp.int32, (TILE_W, LANES), 0).astype(F32) + 0.5

    def kernel_of(centre):
        scaled = (cell - centre) * (40.0 / TILE_W)
        return jnp.exp(-0.5 * (scaled * scaled))

    def add_stars(blocks, first):
        for b in range(RING):
            rows = blocks(b)
            here = rows[4:5] == mine
            rows_y, rows_x = kernel_of(rows[2:3]), kernel_of(rows[3:4])
            lanes = slice(b * LANES, (b + 1) * LANES)
            left[0:TILE_W, lanes] = (jnp.where(here, rows[0:1], 0.0) * rows_y).astype(BF16)
            left[TILE_W:, lanes] = (jnp.where(here, rows[1:2], 0.0) * rows_y).astype(BF16)
            right[:, lanes] = rows_x.astype(BF16)
        out = lax.dot_general(left[...], right[...], (((1,), (1,)), ((), ())), preferred_element_type=F32)
        out = out.reshape(2, 1, TILE_W, TILE_W)
        if first:
            image_ref[...] = out
        else:
            image_ref[...] += out

    add_stars(lambda b: spread[b], True)
    for k in range(1, RING):
        deposit_x[k - 1].wait_recv()

    def deposit_step(k, carry):
        add_stars(lambda b: gathered[k, b], False)
        return carry

    lax.fori_loop(1, RING, deposit_step, 0)
    for sent in (to_y, to_z, to_x, back_x, around_y, deposit_z, deposit_x):
        for one in sent:
            one.wait_send()


def shards(*arrays):
    stars = SRC * RING**3
    stage_count = 7
    vmem = pl.BlockSpec(memory_space=pltpu.VMEM)
    return pl.pallas_call(
        functools.partial(kernel, 1.0 / stars, float(stars) ** (-2.0 / 3.0)),
        out_shape=(
            jax.ShapeDtypeStruct((12, ACT), F32),
            jax.ShapeDtypeStruct((2, 1, TILE_W, TILE_W), F32),
        ),
        in_specs=[vmem] * len(arrays),
        out_specs=(vmem, vmem),
        scratch_shapes=[
            pltpu.VMEM((RING, 8, SRC), F32),
            pltpu.VMEM((16, LANES), F32),
            pltpu.VMEM((24, LANES), F32),
            pltpu.VMEM((RING, 24, LANES), F32),
            pltpu.VMEM((16, LANES), F32),
            pltpu.VMEM((RING, 8, LANES), F32),
            pltpu.VMEM((LANES, RING * SRC), BF16),
            pltpu.VMEM((LANES, RING * SRC), BF16),
            pltpu.VMEM((2, RING * SRC, LANES), BF16),
            pltpu.VMEM((RING * LANES, LANES), BF16),
            pltpu.VMEM((RING * LANES, LANES), F32),
            pltpu.VMEM((RING, 8, LANES), F32),
            pltpu.VMEM((RING, 8, LANES), F32),
            pltpu.VMEM((8, LANES), F32),
            pltpu.VMEM((RING, 8, LANES), F32),
            pltpu.VMEM((RING, 8, LANES), F32),
            pltpu.VMEM((RING, RING, 8, LANES), F32),
            pltpu.VMEM((2 * TILE_W, RING * LANES), BF16),
            pltpu.VMEM((TILE_W, RING * LANES), BF16),
            pltpu.SemaphoreType.DMA((stage_count, RING)),
            pltpu.SemaphoreType.DMA((stage_count, RING)),
        ],
        compiler_params=pltpu.CompilerParams(
            collective_id=0, has_side_effects=True, vmem_limit_bytes=48 << 20
        ),
        name="cluster_step",
    )(*arrays)


def solution(mesh):
    both = ("team", "loop")
    columns, rows = P(None, both), P(both)
    return jax.shard_map(
        shards,
        mesh=mesh,
        in_specs=(columns, columns, rows, columns, rows, rows, rows, columns),
        out_specs=(columns, P(None, both, None, None)),
        check_vma=False,
    )
```

```python
import functools
import math

import jax
import jax.numpy as jnp
from jax import lax
from jax.experimental import pallas as pl
from jax.experimental.pallas import tpu as pltpu
from jax.sharding import PartitionSpec as P

MESH = pl.DeviceIdType.MESH
F32, BF16 = jnp.float32, jnp.bfloat16
RING = 8
SRC = 512
ACT = 16
LANES = 128
TILE_W = 128


def split3(v):
    a = v.astype(BF16)
    r = v - a.astype(F32)
    b = r.astype(BF16)
    return a, b, (r - b.astype(F32)).astype(BF16)


def wide3(v):
    return [p.astype(F32) for p in split3(v)]


def wide2(v):
    a = v.astype(BF16).astype(F32)
    return a, (v - a).astype(BF16).astype(F32)


def coarse(v):
    return jnp.round(v * 32.0) * (1.0 / 32.0)


def pad_rows(v, rows):
    gap = jnp.zeros((rows - v.shape[0], v.shape[1]), v.dtype)
    return jnp.concatenate([v, gap], axis=0)


def features(pos, vel, soften):
    h, u = coarse(pos), coarse(vel)
    l, m = pos - h, vel - u
    l1, l2 = wide2(l)
    m1, m2 = wide2(m)
    total = lambda v: jnp.sum(v, axis=0, keepdims=True)
    hh = wide3(total(h * h))
    hl = wide3(total(2.0 * h * l + l * l) + (0.0 if soften is None else soften))
    hu = wide3(total(h * u))
    hm = wide3(total(h * m + l * u + l * m))
    ones = [jnp.ones_like(h)]
    if soften is None:
        near = [h] + hh + ones + [h, h, l1, l2, l1, l1, l2] + hl + ones
        dots = [h, u] + hu + ones + [h, h, m1, m2, l1, l2, u, u, l1, l1, l2, m1, m1, m2] + hm + ones
    else:
        near = [-2.0 * h] + ones + hh
        near += [-2.0 * l1, -2.0 * l2, -2.0 * h, -2.0 * h, -2.0 * l1, -2.0 * l2, -2.0 * l1] + ones + hl
        dots = [-u, -h] + ones + hu
        dots += [-m1, -m2, -h, -h, -u, -u, -l1, -l2, -m1, -m2, -m1, -l1, -l2, -l1] + ones + hm
    near = jnp.concatenate(near, axis=0)
    return near.shape[0], pad_rows(jnp.concatenate([near] + dots, axis=0), LANES)


def correct(targets, force, old_accel, level):
    step = jnp.exp2(-level)
    gap = old_accel[0:3] - force[0:3]
    first = -6.0 * gap - step * (4.0 * old_accel[3:6] + 2.0 * force[3:6])
    second = 12.0 * gap + 6.0 * step * (old_accel[3:6] + force[3:6])
    pos = targets[0:3] + step * step * (first / 24.0 + second / 120.0)
    vel = targets[3:6] + step * (first / 6.0 + second / 24.0)
    return jnp.concatenate([pos, vel, force], axis=0)

STEPS = (0, 1, 7, 2, 6, 3, 5, 4)
GROUPS = ((0, 1), (1, 5), (5, 8))


def kernel(
    gravity, soften,
    pos_in, vel_in, mass_in, old_in, index_in, level_in, tile_in, offset_in,
    state_ref, image_ref,
    pos_ref, vel_ref, mass_ref, old_ref, index_ref, level_ref, tile_ref, offset_ref,
    source, small, own, own_in, rest, rest_in, settled, targets, source_f, moments, near_f, dots_f,
    part, part_in, half, half_in, spread, gathered, tiles, tiles_all, left, right,
    load_sem, send_sem, recv_sem,
):
    team, loop = lax.axis_index("team"), lax.axis_index("loop")
    zh, y, c = team // 16, (team // 2) % 8, team % 2
    zl, x = loop // 4, loop % 4
    z = zh * 2 + zl

    def at(y, z, x, c):
        return ((z // 2) * 16 + y * 2 + c, (z % 2) * 4 + x)

    def y_peer(s):
        return at((y + STEPS[s]) % 8, z, x, c)

    def z_peer(s):
        return at(y, (z + STEPS[s]) % 8, x, c)

    def x_peer(s, sign=1):
        return at(y, z, (x + 4 + sign * (s // 2)) % 4, (c + s % 2) % 2)

    slots = range(1, RING)
    barrier = pltpu.get_barrier_semaphore()
    for s in reversed(slots):
        for peer in (y_peer(s), z_peer(s), x_peer(s)):
            pl.semaphore_signal(barrier, inc=1, device_id=peer, device_id_type=MESH)
    loads = [
        pltpu.make_async_copy(src, dst, load_sem.at[i])
        for i, (src, dst) in enumerate(
            (
                (pos_in, pos_ref), (vel_in, vel_ref), (mass_in, mass_ref), (index_in, index_ref),
                (old_in, old_ref), (level_in, level_ref), (tile_in, tile_ref), (offset_in, offset_ref),
            )
        )
    ]
    for one in loads:
        one.start()
    for one in loads:
        one.wait()

    def copy(stage, slot, src, dst, peer):
        return pltpu.make_async_remote_copy(
            src_ref=src,
            dst_ref=dst,
            send_sem=send_sem.at[stage],
            recv_sem=recv_sem.at[stage, slot],
            device_id=peer,
            device_id_type=MESH,
        )

    def await_all(stage, ref):
        copy(stage, 0, ref, ref, y_peer(1)).wait_recv()

    def await_sent(stage, ref):
        copy(stage, 0, ref, ref, y_peer(1)).wait_send()

    source[0, 0:3, :] = pos_ref[...]
    source[0, 3:6, :] = vel_ref[...]
    source[0, 6:7, :] = mass_ref[...].reshape(1, SRC)
    source[0, 7:8, :] = jnp.zeros((1, SRC), F32)
    small[...] = jnp.zeros_like(small)
    small[0:6, 0:ACT] = old_ref[...]
    small[6:7, 0:ACT] = level_ref[...].reshape(1, ACT).astype(F32)
    small[7:8, 0:ACT] = tile_ref[...].reshape(1, ACT).astype(F32)
    small[8:10, 0:ACT] = offset_ref[...].astype(F32)
    small[10:11, 0:ACT] = index_ref[...].reshape(1, ACT).astype(F32)
    placed = pltpu.roll(small[...], y * ACT, 1)
    star = lax.broadcasted_iota(jnp.int32, (SRC, LANES), 0).astype(F32)
    lane = lax.broadcasted_iota(jnp.int32, (SRC, LANES), 1)
    chosen = jnp.where((star == placed[10:11]) & (lane // ACT == y), 1.0, 0.0).astype(BF16)
    pieces = jnp.concatenate(wide3(source[0]), axis=0).astype(BF16)
    picked = jnp.dot(pieces, chosen, preferred_element_type=F32)
    own[...] = picked[0:8] + picked[8:16] + picked[16:24]
    rest[...] = placed

    pl.semaphore_wait(barrier, 3 * (RING - 1))

    for s in reversed(slots):
        copy(0, 0, own, own_in.at[s - 1], y_peer(s)).start()
    for s in reversed(slots):
        copy(2, s, source.at[0], source.at[s], z_peer(s)).start()
    for s in slots:
        copy(1, 0, rest, rest_in.at[s - 1], y_peer(s)).start()

    def prepare_source(s):
        v = source[s]
        rows = slice(s * SRC, (s + 1) * SRC)
        source_f[rows, :] = jnp.transpose(features(v[0:3], v[3:6], None)[1]).astype(BF16)
        mass = v[6:7]
        sums = jnp.concatenate([v[0:3] * mass, v[3:6] * mass, mass, jnp.zeros_like(mass)], axis=0)
        moments[:, rows] = pad_rows(jnp.concatenate(wide3(sums), axis=0), 32).astype(BF16)

    def await_source(s):
        copy(2, s, source.at[0], source.at[s], z_peer(s)).wait_recv()

    prepare_source(0)
    for s in range(1, 5):
        await_source(s)
        prepare_source(s)

    await_all(0, own_in)
    block = own[...]
    for s in slots:
        block = block + own_in[s - 1]
    targets[0] = block
    for s in (4, 5, 2, 3, 6, 7, 1):
        copy(3, s, targets.at[0], targets.at[s], x_peer(s)).start()

    def prepare_targets(first, last):
        t = jnp.concatenate([targets[s] for s in range(first, last)], axis=1)
        cut, f = features(t[0:3], t[3:6], soften)
        row = lax.broadcasted_iota(jnp.int32, f.shape, 0)
        lanes = slice(first * LANES, last * LANES)
        near_f[:, lanes] = jnp.where(row < cut, f, 0.0).astype(BF16)
        dots_f[:, lanes] = jnp.where(row < cut, 0.0, f).astype(BF16)

    prepare_targets(0, 1)
    for s in range(5, RING):
        await_source(s)
        prepare_source(s)

    def forces(s):
        lanes = pl.ds(pl.multiple_of(s * LANES, LANES), LANES)
        dist_sq = jnp.dot(source_f[...], near_f[:, lanes], preferred_element_type=F32)
        dots = jnp.dot(source_f[...], dots_f[:, lanes], preferred_element_type=F32)
        inverse = lax.rsqrt(dist_sq)
        inverse_sq = inverse * inverse
        strength = inverse * inverse_sq
        radial = (strength * inverse_sq) * dots
        plain = jnp.dot(moments[...], strength.astype(BF16), preferred_element_type=F32)
        tilted = jnp.dot(moments[...], radial.astype(BF16), preferred_element_type=F32)
        plain = plain[0:8] + plain[8:16] + plain[16:24]
        tilted = tilted[0:8] + tilted[8:16] + tilted[16:24]
        t = targets[s]
        accel = plain[0:3] - t[0:3] * plain[6:7]
        jerk = (plain[3:6] - t[3:6] * plain[6:7]) - 3.0 * (tilted[0:3] - t[0:3] * tilted[6:7])
        part[s] = pad_rows(gravity * jnp.concatenate([accel, jerk], axis=0), 8)

    forces(0)

    await_all(1, rest_in)
    others = rest[...]
    for s in slots:
        others = others + rest_in[s - 1]
    settled[...] = others
    tiles[0] = others[7:8]
    for s in slots:
        copy(10, 0, tiles.at[0], tiles.at[s], z_peer(s)).start()

    for s in slots:
        copy(3, s, targets.at[0], targets.at[s], x_peer(s)).wait_recv()
    prepare_targets(1, RING)

    def force_step(i, carry):
        s = jnp.where(i == 7, 1, jnp.where(i < 3, i + 3, jnp.where(i < 5, i - 1, i + 1)))
        forces(s)
        copy(4, s, part.at[s], part_in.at[s], x_peer(s, -1)).start()
        return carry

    lax.fori_loop(1, RING, force_step, 0)

    await_all(10, tiles.at[pl.ds(1, RING - 1)])
    for s in slots:
        copy(11, 0, tiles, tiles_all.at[s - 1], x_peer(s)).start()

    total = part[0]
    for s in (4, 5, 2, 3, 6, 7, 1):
        copy(4, s, part.at[s], part_in.at[s], x_peer(s, -1)).wait_recv()
        total = total + part_in[s]
    half[...] = total
    for s in reversed(slots):
        copy(5, 0, half, half_in.at[s - 1], y_peer(s)).start()
    await_sent(0, own_in)
    await_sent(1, rest_in)
    await_sent(2, source.at[pl.ds(1, RING - 1)])
    await_sent(3, targets.at[pl.ds(1, RING - 1)])
    await_sent(4, part.at[pl.ds(1, RING - 1)])
    await_sent(10, tiles.at[pl.ds(1, RING - 1)])
    await_sent(11, tiles_all)
    await_all(11, tiles_all)
    await_all(5, half_in)
    for s in slots:
        total = total + half_in[s - 1]

    stars = targets[0]
    others = settled[...]
    state = correct(stars[0:6], total[0:6], others[0:6], others[6:7])
    centre_y = others[8:9] + (TILE_W / 16.0) * jnp.tanh(state[1:2])
    centre_x = others[9:10] + (TILE_W / 16.0) * jnp.tanh(state[0:1])
    mass = stars[6:7]
    spread[0] = jnp.concatenate([mass, mass * state[5:6] * state[5:6], centre_y, centre_x], axis=0)
    for s in reversed(slots):
        copy(6, s, spread.at[0], spread.at[s], z_peer(s)).start()

    def group(g, s, peer):
        low, high = GROUPS[g]
        piece = pl.ds(low, high - low)
        return copy(7 + g, s, spread.at[piece], gathered.at[s, piece], peer)

    def forward(g):
        for s in (4, 5, 2, 3, 6, 7, 1):
            group(g, s, x_peer(s)).start()

    def await_spread(low, high):
        for s in range(low, high):
            copy(6, s, spread.at[0], spread.at[s], z_peer(s)).wait_recv()

    mine = (team * 8 + loop).astype(F32)
    reach = (40.0 / TILE_W) * math.sqrt(0.5 * math.log2(math.e))
    cell = (lax.broadcasted_iota(jnp.int32, (TILE_W, LANES), 0).astype(F32) + 0.5) * reach

    def kernel_of(centre):
        scaled = cell - centre * reach
        return jnp.exp2(-(scaled * scaled))

    def add_stars(blocks, first=False):
        for b, (rows, tile) in enumerate(blocks):
            here = tile == mine
            rows_y, rows_x = kernel_of(rows[2:3]), kernel_of(rows[3:4])
            lanes = slice(b * LANES, (b + 1) * LANES)
            left[0:TILE_W, lanes] = (jnp.where(here, rows[0:1], 0.0) * rows_y).astype(BF16)
            left[TILE_W:, lanes] = (jnp.where(here, rows[1:2], 0.0) * rows_y).astype(BF16)
            right[:, lanes] = rows_x.astype(BF16)
        depth = len(blocks) * LANES
        out = lax.dot_general(
            left[:, 0:depth], right[:, 0:depth], (((1,), (1,)), ((), ())), preferred_element_type=F32
        ).reshape(2, 1, TILE_W, TILE_W)
        if first:
            image_ref[...] = out
        else:
            image_ref[...] += out

    def mine_of(low, high):
        return [(spread[s], tiles[s]) for s in range(low, high)]

    forward(0)
    shifted = pltpu.roll(pad_rows(state, 16), (LANES - y * ACT) % LANES, 1)
    state_ref[...] = shifted[0:12, 0:ACT]
    add_stars(mine_of(0, 1), True)
    await_spread(1, 5)
    forward(1)
    add_stars(mine_of(1, 5))
    await_spread(5, RING)
    forward(2)
    add_stars(mine_of(5, RING))
    for s in (1, 2, 3, 6, 7, 4, 5):
        group(0, s, x_peer(s)).wait_recv()
    add_stars([(gathered[s, 0], tiles_all[s - 1, 0]) for s in slots])

    def deposit_step(g):
        low, high = GROUPS[g]

        def step(s, carry):
            group(g, s, x_peer(s)).wait_recv()
            add_stars([(gathered[s, k], tiles_all[s - 1, k]) for k in range(low, high)])
            return carry

        return step

    lax.fori_loop(1, RING, deposit_step(1), 0)
    lax.fori_loop(1, RING, deposit_step(2), 0)
    await_sent(5, half_in)
    await_sent(6, spread.at[pl.ds(1, RING - 1)])
    for g, (low, high) in enumerate(GROUPS):
        await_sent(7 + g, gathered.at[pl.ds(1, RING - 1), pl.ds(low, high - low)])


def shards(*arrays):
    stars = SRC * RING**3
    stage_count = 12
    vmem = pl.BlockSpec(memory_space=pltpu.VMEM)
    return pl.pallas_call(
        functools.partial(kernel, 1.0 / stars, float(stars) ** (-2.0 / 3.0)),
        out_shape=(
            jax.ShapeDtypeStruct((12, ACT), F32),
            jax.ShapeDtypeStruct((2, 1, TILE_W, TILE_W), F32),
        ),
        in_specs=[pl.BlockSpec(memory_space=pl.ANY)] * len(arrays),
        out_specs=(vmem, vmem),
        scratch_shapes=[pltpu.VMEM(v.shape, v.dtype) for v in arrays] + [
            pltpu.VMEM((RING, 8, SRC), F32),
            pltpu.VMEM((16, LANES), F32),
            pltpu.VMEM((8, LANES), F32),
            pltpu.VMEM((RING - 1, 8, LANES), F32),
            pltpu.VMEM((16, LANES), F32),
            pltpu.VMEM((RING - 1, 16, LANES), F32),
            pltpu.VMEM((16, LANES), F32),
            pltpu.VMEM((RING, 8, LANES), F32),
            pltpu.VMEM((RING * SRC, LANES), BF16),
            pltpu.VMEM((32, RING * SRC), BF16),
            pltpu.VMEM((LANES, RING * LANES), BF16),
            pltpu.VMEM((LANES, RING * LANES), BF16),
            pltpu.VMEM((RING, 8, LANES), F32),
            pltpu.VMEM((RING, 8, LANES), F32),
            pltpu.VMEM((8, LANES), F32),
            pltpu.VMEM((RING - 1, 8, LANES), F32),
            pltpu.VMEM((RING, 4, LANES), F32),
            pltpu.VMEM((RING, RING, 4, LANES), F32),
            pltpu.VMEM((RING, 1, LANES), F32),
            pltpu.VMEM((RING - 1, RING, 1, LANES), F32),
            pltpu.VMEM((2 * TILE_W, RING * LANES), BF16),
            pltpu.VMEM((TILE_W, RING * LANES), BF16),
            pltpu.SemaphoreType.DMA((len(arrays),)),
            pltpu.SemaphoreType.DMA((stage_count,)),
            pltpu.SemaphoreType.DMA((stage_count, RING)),
        ],
        compiler_params=pltpu.CompilerParams(
            collective_id=0, has_side_effects=True, vmem_limit_bytes=60 << 20
        ),
        name="cluster_step",
    )(*arrays)


def solution(mesh):
    both = ("team", "loop")
    columns, rows = P(None, both), P(both)
    return jax.shard_map(
        shards,
        mesh=mesh,
        in_specs=(columns, columns, rows, columns, rows, rows, rows, columns),
        out_specs=(columns, P(None, both, None, None)),
        check_vma=False,
    )
```

```python
import functools
import math

import jax
import jax.numpy as jnp
from jax import lax
from jax.experimental import pallas as pl
from jax.experimental.pallas import tpu as pltpu
from jax.sharding import PartitionSpec as P

MESH = pl.DeviceIdType.MESH
F32, BF16 = jnp.float32, jnp.bfloat16
RING = 8
SRC = 512
ACT = 16
LANES = 128
TILE_W = 128


def split3(v):
    a = v.astype(BF16)
    r = v - a.astype(F32)
    b = r.astype(BF16)
    return a, b, (r - b.astype(F32)).astype(BF16)


def wide3(v):
    return [p.astype(F32) for p in split3(v)]


def wide2(v):
    a = v.astype(BF16).astype(F32)
    return a, (v - a).astype(BF16).astype(F32)


def coarse(v):
    return jnp.round(v * 32.0) * (1.0 / 32.0)


def pad_rows(v, rows):
    gap = jnp.zeros((rows - v.shape[0], v.shape[1]), v.dtype)
    return jnp.concatenate([v, gap], axis=0)


def features(pos, vel, soften):
    h, u = coarse(pos), coarse(vel)
    l, m = pos - h, vel - u
    l1, l2 = wide2(l)
    m1, m2 = wide2(m)
    total = lambda v: jnp.sum(v, axis=0, keepdims=True)
    hh = wide3(total(h * h))
    hl = wide3(total(2.0 * h * l + l * l) + (0.0 if soften is None else soften))
    hu = wide3(total(h * u))
    hm = wide3(total(h * m + l * u + l * m))
    ones = [jnp.ones_like(h)]
    if soften is None:
        near = [h] + hh + ones + [h, h, l1, l2, l1, l1, l2] + hl + ones
        dots = [h, u] + hu + ones + [h, h, m1, m2, l1, l2, u, u, l1, l1, l2, m1, m1, m2] + hm + ones
    else:
        near = [-2.0 * h] + ones + hh
        near += [-2.0 * l1, -2.0 * l2, -2.0 * h, -2.0 * h, -2.0 * l1, -2.0 * l2, -2.0 * l1] + ones + hl
        dots = [-u, -h] + ones + hu
        dots += [-m1, -m2, -h, -h, -u, -u, -l1, -l2, -m1, -m2, -m1, -l1, -l2, -l1] + ones + hm
    near = jnp.concatenate(near, axis=0)
    return near.shape[0], pad_rows(jnp.concatenate([near] + dots, axis=0), LANES)


def correct(targets, force, old_accel, level):
    step = jnp.exp2(-level)
    gap = old_accel[0:3] - force[0:3]
    first = -6.0 * gap - step * (4.0 * old_accel[3:6] + 2.0 * force[3:6])
    second = 12.0 * gap + 6.0 * step * (old_accel[3:6] + force[3:6])
    pos = targets[0:3] + step * step * (first / 24.0 + second / 120.0)
    vel = targets[3:6] + step * (first / 6.0 + second / 24.0)
    return jnp.concatenate([pos, vel, force], axis=0)

PAIR = 2
EARLY = 5


def kernel(
    gravity, soften,
    pos_in, vel_in, mass_in, old_in, index_in, level_in, tile_in, offset_in,
    state_ref, image_ref,
    pos_ref, vel_ref, mass_ref, old_ref, index_ref, level_ref, tile_ref, offset_ref,
    source, small, own, own_in, rest, rest_in, settled, targets, source_f, moments, near_f, dots_f,
    part, part_in, half, half_in, spread, gathered, tiles, tiles_all, left, right,
    load_sem, send_sem, recv_sem,
):
    team, loop = lax.axis_index("team"), lax.axis_index("loop")
    zh, y, c = team // 16, (team // 2) % 8, team % 2
    zl, x = loop // 4, loop % 4
    z = zh * 2 + zl

    def at(y, z, x, c):
        return ((z // 2) * 16 + y * 2 + c, (z % 2) * 4 + x)

    def step_of(s):
        away = (s + 1) // 2
        return away + (s + 1) % 2 * (8 - 2 * away)

    def y_peer(s, sign=1):
        return at((y + 8 + sign * step_of(s)) % 8, z, x, c)

    def z_peer(s):
        return at(y, (z + step_of(s)) % 8, x, c)

    def x_peer(s):
        return at(y, z, (x + s // 2) % 4, (c + s % 2) % 2)

    slots = range(1, RING)
    barrier = pltpu.get_barrier_semaphore()
    for s in reversed(slots):
        for peer in (y_peer(s), z_peer(s), x_peer(s)):
            pl.semaphore_signal(barrier, inc=1, device_id=peer, device_id_type=MESH)
    loads = [
        pltpu.make_async_copy(src, dst, load_sem.at[i])
        for i, (src, dst) in enumerate(
            (
                (pos_in, pos_ref), (vel_in, vel_ref), (mass_in, mass_ref), (index_in, index_ref),
                (old_in, old_ref), (level_in, level_ref), (tile_in, tile_ref), (offset_in, offset_ref),
            )
        )
    ]
    for one in loads:
        one.start()
    for one in loads:
        one.wait()

    def copy(stage, slot, src, dst, peer):
        return pltpu.make_async_remote_copy(
            src_ref=src,
            dst_ref=dst,
            send_sem=send_sem.at[stage],
            recv_sem=recv_sem.at[stage, slot],
            device_id=peer,
            device_id_type=MESH,
        )

    def await_all(stage, ref):
        copy(stage, 0, ref, ref, y_peer(1)).wait_recv()

    def await_sent(stage, ref):
        copy(stage, 0, ref, ref, y_peer(1)).wait_send()

    source[0, 0:3, :] = pos_ref[...]
    source[0, 3:6, :] = vel_ref[...]
    source[0, 6:7, :] = mass_ref[...].reshape(1, SRC)
    source[0, 7:8, :] = jnp.zeros((1, SRC), F32)
    small[...] = jnp.zeros_like(small)
    small[0:6, 0:ACT] = old_ref[...]
    small[6:7, 0:ACT] = level_ref[...].reshape(1, ACT).astype(F32)
    small[7:8, 0:ACT] = tile_ref[...].reshape(1, ACT).astype(F32)
    small[8:10, 0:ACT] = offset_ref[...].astype(F32)
    small[10:11, 0:ACT] = index_ref[...].reshape(1, ACT).astype(F32)
    place = x * 2 + c
    placed = pltpu.roll(small[...], place * ACT, 1)
    star = lax.broadcasted_iota(jnp.int32, (SRC, LANES), 0).astype(F32)
    lane = lax.broadcasted_iota(jnp.int32, (SRC, LANES), 1)
    chosen = jnp.where((star == placed[10:11]) & (lane // ACT == place), 1.0, 0.0).astype(BF16)
    pieces = jnp.concatenate(wide3(source[0]), axis=0).astype(BF16)
    picked = jnp.dot(pieces, chosen, preferred_element_type=F32)
    own[...] = picked[0:8] + picked[8:16] + picked[16:24]
    rest[...] = placed

    pl.semaphore_wait(barrier, 3 * (RING - 1))

    for s in (4, 5, 2, 3, 6, 7, 1):
        copy(0, 0, own, own_in.at[s - 1], x_peer(s)).start()
    for s in reversed(slots):
        copy(2, s, source.at[0], source.at[s], z_peer(s)).start()
    for s in slots:
        copy(1, 0, rest, rest_in.at[s - 1], x_peer(s)).start()

    def prepare_source(s):
        v = source[s]
        rows = slice(s * SRC, (s + 1) * SRC)
        source_f[rows, :] = jnp.transpose(features(v[0:3], v[3:6], None)[1]).astype(BF16)
        mass = v[6:7]
        sums = jnp.concatenate([v[0:3] * mass, v[3:6] * mass, mass, jnp.zeros_like(mass)], axis=0)
        moments[:, rows] = pad_rows(jnp.concatenate(wide3(sums), axis=0), 32).astype(BF16)

    def await_source(s):
        copy(2, s, source.at[0], source.at[s], z_peer(s)).wait_recv()

    def prepare_targets(first, last):
        t = jnp.concatenate([targets[s] for s in range(first, last)], axis=1)
        cut, f = features(t[0:3], t[3:6], soften)
        row = lax.broadcasted_iota(jnp.int32, f.shape, 0)
        lanes = slice(first * LANES, last * LANES)
        near_f[:, lanes] = jnp.where(row < cut, f, 0.0).astype(BF16)
        dots_f[:, lanes] = jnp.where(row < cut, 0.0, f).astype(BF16)

    def force_sums(s, first, last):
        lanes = pl.ds(pl.multiple_of(s * LANES, LANES), LANES)
        rows = slice(first * SRC, last * SRC)
        dist_sq = jnp.dot(source_f[rows, :], near_f[:, lanes], preferred_element_type=F32)
        dots = jnp.dot(source_f[rows, :], dots_f[:, lanes], preferred_element_type=F32)
        inverse = lax.rsqrt(dist_sq)
        inverse_sq = inverse * inverse
        strength = inverse * inverse_sq
        radial = (strength * inverse_sq) * dots
        plain = jnp.dot(moments[:, rows], strength.astype(BF16), preferred_element_type=F32)
        tilted = jnp.dot(moments[:, rows], radial.astype(BF16), preferred_element_type=F32)
        return plain[0:8] + plain[8:16] + plain[16:24], tilted[0:8] + tilted[8:16] + tilted[16:24]

    def combine(s, plain, tilted):
        t = targets[s]
        accel = plain[0:3] - t[0:3] * plain[6:7]
        jerk = (plain[3:6] - t[3:6] * plain[6:7]) - 3.0 * (tilted[0:3] - t[0:3] * tilted[6:7])
        part[s] = pad_rows(gravity * jnp.concatenate([accel, jerk], axis=0), 8)

    prepare_source(0)

    await_all(0, own_in)
    block = own[...]
    for s in slots:
        block = block + own_in[s - 1]
    targets[0] = block
    for s in reversed(slots):
        copy(3, s, targets.at[0], targets.at[s], y_peer(s)).start()
    prepare_targets(0, 1)
    for s in range(1, EARLY):
        await_source(s)
        prepare_source(s)
    plain, tilted = force_sums(0, 0, EARLY)

    await_all(1, rest_in)
    others = rest[...]
    for s in slots:
        others = others + rest_in[s - 1]
    settled[...] = others
    tiles[0] = others[7:8]
    for s in slots:
        copy(11, 0, tiles.at[0], tiles.at[s], z_peer(s)).start()
    image_ref[...] = jnp.zeros_like(image_ref)

    for s in range(EARLY, RING):
        await_source(s)
        prepare_source(s)
    more = force_sums(0, EARLY, RING)
    combine(0, plain + more[0], tilted + more[1])

    def await_targets(s):
        copy(3, s, targets.at[0], targets.at[s], y_peer(s)).wait_recv()

    def force_step(i, carry):
        @pl.when(i == 0)
        def _():
            await_targets(1)
            prepare_targets(1, 2)

        @pl.when(i == 1)
        def _():
            await_targets(3)
            prepare_targets(3, 4)

        @pl.when(i == 2)
        def _():
            for s in (2, 4, 5, 6, 7):
                await_targets(s)
            prepare_targets(4, RING)
            prepare_targets(2, 3)

        s = jnp.where(i < 2, 2 * i + 1, jnp.where(i == 2, 7, jnp.where(i == 3, 5, 14 - 2 * i)))
        combine(s, *force_sums(s, 0, RING))
        copy(4, s, part.at[s], part_in.at[s], y_peer(s, -1)).start()
        return carry

    lax.fori_loop(0, RING - 1, force_step, 0)

    await_all(11, tiles.at[pl.ds(1, RING - 1)])
    for s in slots:
        copy(12, 0, tiles, tiles_all.at[s - 1], y_peer(s)).start()

    total = part[0]
    for s in (1, 3, 7, 5, 6, 4, 2):
        copy(4, s, part.at[s], part_in.at[s], y_peer(s, -1)).wait_recv()
        total = total + part_in[s]
    half[...] = total
    for s in (4, 5, 2, 3, 6, 7, 1):
        copy(5, 0, half, half_in.at[s - 1], x_peer(s)).start()
    await_sent(0, own_in)
    await_sent(1, rest_in)
    await_sent(2, source.at[pl.ds(1, RING - 1)])
    await_sent(3, targets.at[pl.ds(1, RING - 1)])
    await_sent(4, part.at[pl.ds(1, RING - 1)])
    await_sent(11, tiles.at[pl.ds(1, RING - 1)])
    await_sent(12, tiles_all)
    await_all(12, tiles_all)
    await_all(5, half_in)
    for s in slots:
        total = total + half_in[s - 1]

    stars = targets[0]
    others = settled[...]
    state = correct(stars[0:6], total[0:6], others[0:6], others[6:7])
    centre_y = others[8:9] + (TILE_W / 16.0) * jnp.tanh(state[1:2])
    centre_x = others[9:10] + (TILE_W / 16.0) * jnp.tanh(state[0:1])
    mass = stars[6:7]
    spread[0] = jnp.concatenate([mass, mass * state[5:6] * state[5:6], centre_y, centre_x], axis=0)
    for s in reversed(slots):
        copy(6, s, spread.at[0], spread.at[s], z_peer(s)).start()

    def pair(g, s, peer):
        piece = pl.ds(g * PAIR, PAIR)
        return copy(7 + g, s, spread.at[piece], gathered.at[s, piece], peer)

    mine = (team * 8 + loop).astype(F32)
    reach = (40.0 / TILE_W) * math.sqrt(0.5 * math.log2(math.e))
    cell = (lax.broadcasted_iota(jnp.int32, (TILE_W, LANES), 0).astype(F32) + 0.5) * reach

    def kernel_of(centre):
        scaled = cell - centre * reach
        return jnp.exp2(-(scaled * scaled))

    def add_stars(blocks):
        for b, (rows, tile) in enumerate(blocks):
            here = tile == mine
            rows_y, rows_x = kernel_of(rows[2:3]), kernel_of(rows[3:4])
            lanes = slice(b * LANES, (b + 1) * LANES)
            left[0:TILE_W, lanes] = (jnp.where(here, rows[0:1], 0.0) * rows_y).astype(BF16)
            left[TILE_W:, lanes] = (jnp.where(here, rows[1:2], 0.0) * rows_y).astype(BF16)
            right[:, lanes] = rows_x.astype(BF16)
        out = lax.dot_general(
            left[...], right[...], (((1,), (1,)), ((), ())), preferred_element_type=F32
        )
        image_ref[...] += out.reshape(2, 1, TILE_W, TILE_W)

    def forward_step(g, carry):
        @pl.when(g == 0)
        def _():
            copy(6, 1, spread.at[0], spread.at[1], z_peer(1)).wait_recv()

        @pl.when(g > 0)
        def _():
            for s in (2 * g, 2 * g + 1):
                copy(6, s, spread.at[0], spread.at[s], z_peer(s)).wait_recv()

        for s in reversed(slots):
            pair(g, s, y_peer(s)).start()
        add_stars([(spread[g * PAIR + k], tiles[g * PAIR + k]) for k in range(PAIR)])
        return carry

    shifted = pltpu.roll(pad_rows(state, 16), (LANES - place * ACT) % LANES, 1)
    state_ref[...] = shifted[0:12, 0:ACT]
    lax.fori_loop(0, RING // PAIR, forward_step, 0)

    def deposit_step(i, carry):
        late, s = i // (RING - 1) + 1, i % (RING - 1) + 1
        g = late - (s + 1) // 2

        @pl.when((g >= 0) & (g < RING // PAIR))
        def _():
            pair(g, s, y_peer(s)).wait_recv()
            add_stars([(gathered[s, g * PAIR + k], tiles_all[s - 1, g * PAIR + k]) for k in range(PAIR)])

        return carry

    lax.fori_loop(0, (RING - 1) * (RING - 1), deposit_step, 0)
    await_sent(5, half_in)
    await_sent(6, spread.at[pl.ds(1, RING - 1)])
    for g in range(RING // PAIR):
        await_sent(7 + g, gathered.at[pl.ds(1, RING - 1), pl.ds(g * PAIR, PAIR)])


def shards(*arrays):
    stars = SRC * RING**3
    stage_count = 13
    vmem = pl.BlockSpec(memory_space=pltpu.VMEM)
    return pl.pallas_call(
        functools.partial(kernel, 1.0 / stars, float(stars) ** (-2.0 / 3.0)),
        out_shape=(
            jax.ShapeDtypeStruct((12, ACT), F32),
            jax.ShapeDtypeStruct((2, 1, TILE_W, TILE_W), F32),
        ),
        in_specs=[pl.BlockSpec(memory_space=pl.ANY)] * len(arrays),
        out_specs=(vmem, vmem),
        scratch_shapes=[pltpu.VMEM(v.shape, v.dtype) for v in arrays] + [
            pltpu.VMEM((RING, 8, SRC), F32),
            pltpu.VMEM((16, LANES), F32),
            pltpu.VMEM((8, LANES), F32),
            pltpu.VMEM((RING - 1, 8, LANES), F32),
            pltpu.VMEM((16, LANES), F32),
            pltpu.VMEM((RING - 1, 16, LANES), F32),
            pltpu.VMEM((16, LANES), F32),
            pltpu.VMEM((RING, 8, LANES), F32),
            pltpu.VMEM((RING * SRC, LANES), BF16),
            pltpu.VMEM((32, RING * SRC), BF16),
            pltpu.VMEM((LANES, RING * LANES), BF16),
            pltpu.VMEM((LANES, RING * LANES), BF16),
            pltpu.VMEM((RING, 8, LANES), F32),
            pltpu.VMEM((RING, 8, LANES), F32),
            pltpu.VMEM((8, LANES), F32),
            pltpu.VMEM((RING - 1, 8, LANES), F32),
            pltpu.VMEM((RING, 4, LANES), F32),
            pltpu.VMEM((RING, RING, 4, LANES), F32),
            pltpu.VMEM((RING, 1, LANES), F32),
            pltpu.VMEM((RING - 1, RING, 1, LANES), F32),
            pltpu.VMEM((2 * TILE_W, PAIR * LANES), BF16),
            pltpu.VMEM((TILE_W, PAIR * LANES), BF16),
            pltpu.SemaphoreType.DMA((len(arrays),)),
            pltpu.SemaphoreType.DMA((stage_count,)),
            pltpu.SemaphoreType.DMA((stage_count, RING)),
        ],
        compiler_params=pltpu.CompilerParams(
            collective_id=0, has_side_effects=True, vmem_limit_bytes=60 << 20
        ),
        name="cluster_step",
    )(*arrays)


def solution(mesh):
    both = ("team", "loop")
    columns, rows = P(None, both), P(both)
    return jax.shard_map(
        shards,
        mesh=mesh,
        in_specs=(columns, columns, rows, columns, rows, rows, rows, columns),
        out_specs=(columns, P(None, both, None, None)),
        check_vma=False,
    )
```

```python
import functools
import math

import jax
import jax.numpy as jnp
from jax import lax
from jax.experimental import pallas as pl
from jax.experimental.pallas import tpu as pltpu
from jax.sharding import PartitionSpec as P

MESH = pl.DeviceIdType.MESH
F32, BF16 = jnp.float32, jnp.bfloat16
RING = 8
SRC = 512
ACT = 16
LANES = 128
TILE_W = 128


def split3(v):
    a = v.astype(BF16)
    r = v - a.astype(F32)
    b = r.astype(BF16)
    return a, b, (r - b.astype(F32)).astype(BF16)


def wide3(v):
    return [p.astype(F32) for p in split3(v)]


def wide2(v):
    a = v.astype(BF16).astype(F32)
    return a, (v - a).astype(BF16).astype(F32)


def coarse(v):
    return jnp.round(v * 32.0) * (1.0 / 32.0)


def pad_rows(v, rows):
    gap = jnp.zeros((rows - v.shape[0], v.shape[1]), v.dtype)
    return jnp.concatenate([v, gap], axis=0)


def features(pos, vel, soften):
    h, u = coarse(pos), coarse(vel)
    l, m = pos - h, vel - u
    l1, l2 = wide2(l)
    m1, m2 = wide2(m)
    total = lambda v: jnp.sum(v, axis=0, keepdims=True)
    hh = wide3(total(h * h))
    hl = wide3(total(2.0 * h * l + l * l) + (0.0 if soften is None else soften))
    hu = wide3(total(h * u))
    hm = wide3(total(h * m + l * u + l * m))
    ones = [jnp.ones_like(h)]
    if soften is None:
        near = [h] + hh + ones + [h, h, l1, l2, l1, l1, l2] + hl + ones
        dots = [h, u] + hu + ones + [h, h, m1, m2, l1, l2, u, u, l1, l1, l2, m1, m1, m2] + hm + ones
    else:
        near = [-2.0 * h] + ones + hh
        near += [-2.0 * l1, -2.0 * l2, -2.0 * h, -2.0 * h, -2.0 * l1, -2.0 * l2, -2.0 * l1] + ones + hl
        dots = [-u, -h] + ones + hu
        dots += [-m1, -m2, -h, -h, -u, -u, -l1, -l2, -m1, -m2, -m1, -l1, -l2, -l1] + ones + hm
    near = jnp.concatenate(near, axis=0)
    return near.shape[0], pad_rows(jnp.concatenate([near] + dots, axis=0), LANES)


def correct(targets, force, old_accel, level):
    step = jnp.exp2(-level)
    gap = old_accel[0:3] - force[0:3]
    first = -6.0 * gap - step * (4.0 * old_accel[3:6] + 2.0 * force[3:6])
    second = 12.0 * gap + 6.0 * step * (old_accel[3:6] + force[3:6])
    pos = targets[0:3] + step * step * (first / 24.0 + second / 120.0)
    vel = targets[3:6] + step * (first / 6.0 + second / 24.0)
    return jnp.concatenate([pos, vel, force], axis=0)

FOUR = 4
EARLY = 5


def kernel(
    gravity, soften,
    pos_in, vel_in, mass_in, old_in, index_in, level_in, tile_in, offset_in,
    state_ref, image_ref,
    pos_ref, vel_ref, mass_ref, old_ref, index_ref, level_ref, tile_ref, offset_ref,
    source, small, own, own_in, rest, rest_in, settled, targets, source_f, moments, near_f, dots_f,
    part, part_in, half, half_in, spread, gathered, tiles, tiles_all, left, right,
    load_sem, send_sem, recv_sem,
):
    team, loop = lax.axis_index("team"), lax.axis_index("loop")
    zh, y, c = team // 16, (team // 2) % 8, team % 2
    zl, x = loop // 4, loop % 4
    z = zh * 2 + zl

    def at(y, z, x, c):
        return ((z // 2) * 16 + y * 2 + c, (z % 2) * 4 + x)

    def step_of(s):
        away = (s + 1) // 2
        return away + (s + 1) % 2 * (8 - 2 * away)

    def y_peer(s, sign=1):
        return at((y + 8 + sign * step_of(s)) % 8, z, x, c)

    def z_peer(s):
        return at(y, (z + step_of(s)) % 8, x, c)

    def x_peer(s):
        return at(y, z, (x + s // 2) % 4, (c + s % 2) % 2)

    slots = range(1, RING)
    barrier = pltpu.get_barrier_semaphore()
    for s in reversed(slots):
        for peer in (y_peer(s), z_peer(s), x_peer(s)):
            pl.semaphore_signal(barrier, inc=1, device_id=peer, device_id_type=MESH)
    loads = [
        pltpu.make_async_copy(src, dst, load_sem.at[i])
        for i, (src, dst) in enumerate(
            (
                (pos_in, pos_ref), (vel_in, vel_ref), (mass_in, mass_ref), (index_in, index_ref),
                (old_in, old_ref), (level_in, level_ref), (tile_in, tile_ref), (offset_in, offset_ref),
            )
        )
    ]
    for one in loads:
        one.start()
    for one in loads:
        one.wait()

    def copy(stage, slot, src, dst, peer):
        return pltpu.make_async_remote_copy(
            src_ref=src,
            dst_ref=dst,
            send_sem=send_sem.at[stage],
            recv_sem=recv_sem.at[stage, slot],
            device_id=peer,
            device_id_type=MESH,
        )

    def await_all(stage, ref):
        copy(stage, 0, ref, ref, y_peer(1)).wait_recv()

    def await_sent(stage, ref):
        copy(stage, 0, ref, ref, y_peer(1)).wait_send()

    source[0, 0:3, :] = pos_ref[...]
    source[0, 3:6, :] = vel_ref[...]
    source[0, 6:7, :] = mass_ref[...].reshape(1, SRC)
    source[0, 7:8, :] = jnp.zeros((1, SRC), F32)
    small[...] = jnp.zeros_like(small)
    small[0:6, 0:ACT] = old_ref[...]
    small[6:7, 0:ACT] = level_ref[...].reshape(1, ACT).astype(F32)
    small[7:8, 0:ACT] = tile_ref[...].reshape(1, ACT).astype(F32)
    small[8:10, 0:ACT] = offset_ref[...].astype(F32)
    small[10:11, 0:ACT] = index_ref[...].reshape(1, ACT).astype(F32)
    place = x * 2 + c
    placed = pltpu.roll(small[...], place * ACT, 1)
    star = lax.broadcasted_iota(jnp.int32, (SRC, LANES), 0).astype(F32)
    lane = lax.broadcasted_iota(jnp.int32, (SRC, LANES), 1)
    chosen = jnp.where((star == placed[10:11]) & (lane // ACT == place), 1.0, 0.0).astype(BF16)
    pieces = jnp.concatenate(wide3(source[0]), axis=0).astype(BF16)
    picked = jnp.dot(pieces, chosen, preferred_element_type=F32)
    own[...] = picked[0:8] + picked[8:16] + picked[16:24]
    rest[...] = placed

    pl.semaphore_wait(barrier, 3 * (RING - 1))

    for s in (4, 5, 2, 3, 6, 7, 1):
        copy(0, 0, own, own_in.at[s - 1], x_peer(s)).start()
    for s in reversed(slots):
        copy(2, s, source.at[0], source.at[s], z_peer(s)).start()
    for s in slots:
        copy(1, 0, rest, rest_in.at[s - 1], x_peer(s)).start()

    def prepare_source(s):
        v = source[s]
        rows = slice(s * SRC, (s + 1) * SRC)
        source_f[rows, :] = jnp.transpose(features(v[0:3], v[3:6], None)[1]).astype(BF16)
        mass = v[6:7]
        sums = jnp.concatenate([v[0:3] * mass, v[3:6] * mass, mass, jnp.zeros_like(mass)], axis=0)
        moments[:, rows] = pad_rows(jnp.concatenate(wide3(sums), axis=0), 32).astype(BF16)

    def await_source(s):
        copy(2, s, source.at[0], source.at[s], z_peer(s)).wait_recv()

    def prepare_targets(first, last):
        t = jnp.concatenate([targets[s] for s in range(first, last)], axis=1)
        cut, f = features(t[0:3], t[3:6], soften)
        row = lax.broadcasted_iota(jnp.int32, f.shape, 0)
        lanes = slice(first * LANES, last * LANES)
        near_f[:, lanes] = jnp.where(row < cut, f, 0.0).astype(BF16)
        dots_f[:, lanes] = jnp.where(row < cut, 0.0, f).astype(BF16)

    def force_sums(s, first, last):
        lanes = pl.ds(pl.multiple_of(s * LANES, LANES), LANES)
        rows = slice(first * SRC, last * SRC)
        dist_sq = jnp.dot(source_f[rows, :], near_f[:, lanes], preferred_element_type=F32)
        dots = jnp.dot(source_f[rows, :], dots_f[:, lanes], preferred_element_type=F32)
        inverse = lax.rsqrt(dist_sq)
        inverse_sq = inverse * inverse
        strength = inverse * inverse_sq
        radial = (strength * inverse_sq) * dots
        plain = jnp.dot(moments[:, rows], strength.astype(BF16), preferred_element_type=F32)
        tilted = jnp.dot(moments[:, rows], radial.astype(BF16), preferred_element_type=F32)
        return plain[0:8] + plain[8:16] + plain[16:24], tilted[0:8] + tilted[8:16] + tilted[16:24]

    def combine(s, plain, tilted):
        t = targets[s]
        accel = plain[0:3] - t[0:3] * plain[6:7]
        jerk = (plain[3:6] - t[3:6] * plain[6:7]) - 3.0 * (tilted[0:3] - t[0:3] * tilted[6:7])
        part[s] = pad_rows(gravity * jnp.concatenate([accel, jerk], axis=0), 8)

    prepare_source(0)

    await_all(0, own_in)
    block = own[...]
    for s in slots:
        block = block + own_in[s - 1]
    targets[0] = block
    for s in reversed(slots):
        copy(3, s, targets.at[0], targets.at[s], y_peer(s)).start()
    prepare_targets(0, 1)
    for s in range(1, EARLY):
        await_source(s)
        prepare_source(s)
    plain, tilted = force_sums(0, 0, EARLY)

    await_all(1, rest_in)
    others = rest[...]
    for s in slots:
        others = others + rest_in[s - 1]
    settled[...] = others
    tiles[0] = others[7:8]
    for s in slots:
        copy(11, 0, tiles.at[0], tiles.at[s], z_peer(s)).start()
    image_ref[...] = jnp.zeros_like(image_ref)

    for s in range(EARLY, RING):
        await_source(s)
        prepare_source(s)
    more = force_sums(0, EARLY, RING)
    combine(0, plain + more[0], tilted + more[1])

    def await_targets(s):
        copy(3, s, targets.at[0], targets.at[s], y_peer(s)).wait_recv()

    def force_step(i, carry):
        @pl.when(i == 0)
        def _():
            await_targets(1)
            prepare_targets(1, 2)

        @pl.when(i == 1)
        def _():
            await_targets(3)
            prepare_targets(3, 4)

        @pl.when(i == 2)
        def _():
            for s in (2, 4, 5, 6, 7):
                await_targets(s)
            prepare_targets(4, RING)
            prepare_targets(2, 3)

        @pl.when(i == 3)
        def _():
            await_all(11, tiles.at[pl.ds(1, RING - 1)])
            for s in slots:
                copy(12, 0, tiles, tiles_all.at[s - 1], y_peer(s)).start()

        s = jnp.where(i < 2, 2 * i + 1, jnp.where(i == 2, 7, jnp.where(i == 3, 5, 14 - 2 * i)))
        combine(s, *force_sums(s, 0, RING))
        copy(4, s, part.at[s], part_in.at[s], y_peer(s, -1)).start()
        return carry

    lax.fori_loop(0, RING - 1, force_step, 0)

    total = part[0]
    for s in (1, 3, 7, 5, 6, 4, 2):
        copy(4, s, part.at[s], part_in.at[s], y_peer(s, -1)).wait_recv()
        total = total + part_in[s]
    half[...] = total
    for s in (4, 5, 2, 3, 6, 7, 1):
        copy(5, 0, half, half_in.at[s - 1], x_peer(s)).start()
    await_sent(0, own_in)
    await_sent(1, rest_in)
    await_sent(2, source.at[pl.ds(1, RING - 1)])
    await_sent(3, targets.at[pl.ds(1, RING - 1)])
    await_sent(4, part.at[pl.ds(1, RING - 1)])
    await_sent(11, tiles.at[pl.ds(1, RING - 1)])
    await_sent(12, tiles_all)
    await_all(12, tiles_all)
    await_all(5, half_in)
    for s in slots:
        total = total + half_in[s - 1]

    stars = targets[0]
    others = settled[...]
    state = correct(stars[0:6], total[0:6], others[0:6], others[6:7])
    centre_y = others[8:9] + (TILE_W / 16.0) * jnp.tanh(state[1:2])
    centre_x = others[9:10] + (TILE_W / 16.0) * jnp.tanh(state[0:1])
    mass = stars[6:7]
    spread[0] = jnp.concatenate([mass, mass * state[5:6] * state[5:6], centre_y, centre_x], axis=0)
    for s in reversed(slots):
        copy(6, s, spread.at[0], spread.at[s], z_peer(s)).start()

    def four(g, s, peer):
        piece = pl.ds(g * FOUR, FOUR)
        return copy(7 + g, s, spread.at[piece], gathered.at[s, piece], peer)

    mine = (team * 8 + loop).astype(F32)
    reach = (40.0 / TILE_W) * math.sqrt(0.5 * math.log2(math.e))
    cell = (lax.broadcasted_iota(jnp.int32, (TILE_W, LANES), 0).astype(F32) + 0.5) * reach

    def kernel_of(centre):
        scaled = cell - centre * reach
        return jnp.exp2(-(scaled * scaled))

    def add_stars(blocks):
        for b, (rows, tile) in enumerate(blocks):
            here = tile == mine
            rows_y, rows_x = kernel_of(rows[2:3]), kernel_of(rows[3:4])
            lanes = slice(b * LANES, (b + 1) * LANES)
            left[0:TILE_W, lanes] = (jnp.where(here, rows[0:1], 0.0) * rows_y).astype(BF16)
            left[TILE_W:, lanes] = (jnp.where(here, rows[1:2], 0.0) * rows_y).astype(BF16)
            right[:, lanes] = rows_x.astype(BF16)
        out = lax.dot_general(
            left[...], right[...], (((1,), (1,)), ((), ())), preferred_element_type=F32
        )
        image_ref[...] += out.reshape(2, 1, TILE_W, TILE_W)

    def forward(g):
        for s in range(max(1, g * FOUR), (g + 1) * FOUR):
            copy(6, s, spread.at[0], spread.at[s], z_peer(s)).wait_recv()
        for s in reversed(slots):
            four(g, s, y_peer(s)).start()
        add_stars([(spread[g * FOUR + k], tiles[g * FOUR + k]) for k in range(FOUR)])

    shifted = pltpu.roll(pad_rows(state, 16), (LANES - place * ACT) % LANES, 1)
    state_ref[...] = shifted[0:12, 0:ACT]
    forward(0)
    forward(1)

    def deposit_step(i, carry):
        g = jnp.where((i < 6) | (i == 8), 0, 1)
        s = jnp.where(i < 6, i + 1, jnp.where(i < 8, i - 5, jnp.where(i == 8, 7, i - 6)))
        four(g, s, y_peer(s)).wait_recv()
        add_stars([(gathered[s, g * FOUR + k], tiles_all[s - 1, g * FOUR + k]) for k in range(FOUR)])
        return carry

    lax.fori_loop(0, 2 * (RING - 1), deposit_step, 0)
    await_sent(5, half_in)
    await_sent(6, spread.at[pl.ds(1, RING - 1)])
    for g in range(RING // FOUR):
        await_sent(7 + g, gathered.at[pl.ds(1, RING - 1), pl.ds(g * FOUR, FOUR)])


def store(state_in, image_in, state_out, image_out, sem):
    copies = [
        pltpu.make_async_copy(state_in, state_out, sem.at[0]),
        pltpu.make_async_copy(image_in, image_out, sem.at[1]),
    ]
    for one in reversed(copies):
        one.start()
    for one in copies:
        one.wait()


def shards(*arrays):
    stars = SRC * RING**3
    stage_count = 13
    vmem = pl.BlockSpec(memory_space=pltpu.VMEM)
    outputs = (
        jax.ShapeDtypeStruct((12, ACT), F32),
        jax.ShapeDtypeStruct((2, 1, TILE_W, TILE_W), F32),
    )
    results = pl.pallas_call(
        functools.partial(kernel, 1.0 / stars, float(stars) ** (-2.0 / 3.0)),
        out_shape=outputs,
        in_specs=[pl.BlockSpec(memory_space=pl.ANY)] * len(arrays),
        out_specs=(vmem, vmem),
        scratch_shapes=[pltpu.VMEM(v.shape, v.dtype) for v in arrays] + [
            pltpu.VMEM((RING, 8, SRC), F32),
            pltpu.VMEM((16, LANES), F32),
            pltpu.VMEM((8, LANES), F32),
            pltpu.VMEM((RING - 1, 8, LANES), F32),
            pltpu.VMEM((16, LANES), F32),
            pltpu.VMEM((RING - 1, 16, LANES), F32),
            pltpu.VMEM((16, LANES), F32),
            pltpu.VMEM((RING, 8, LANES), F32),
            pltpu.VMEM((RING * SRC, LANES), BF16),
            pltpu.VMEM((32, RING * SRC), BF16),
            pltpu.VMEM((LANES, RING * LANES), BF16),
            pltpu.VMEM((LANES, RING * LANES), BF16),
            pltpu.VMEM((RING, 8, LANES), F32),
            pltpu.VMEM((RING, 8, LANES), F32),
            pltpu.VMEM((8, LANES), F32),
            pltpu.VMEM((RING - 1, 8, LANES), F32),
            pltpu.VMEM((RING, 4, LANES), F32),
            pltpu.VMEM((RING, RING, 4, LANES), F32),
            pltpu.VMEM((RING, 1, LANES), F32),
            pltpu.VMEM((RING - 1, RING, 1, LANES), F32),
            pltpu.VMEM((2 * TILE_W, FOUR * LANES), BF16),
            pltpu.VMEM((TILE_W, FOUR * LANES), BF16),
            pltpu.SemaphoreType.DMA((len(arrays),)),
            pltpu.SemaphoreType.DMA((stage_count,)),
            pltpu.SemaphoreType.DMA((stage_count, RING)),
        ],
        compiler_params=pltpu.CompilerParams(
            collective_id=0, has_side_effects=True, vmem_limit_bytes=60 << 20
        ),
        name="cluster_step",
    )(*arrays)
    anywhere = pl.BlockSpec(memory_space=pl.ANY)
    return pl.pallas_call(
        store,
        out_shape=outputs,
        in_specs=[anywhere] * 2,
        out_specs=(anywhere, anywhere),
        scratch_shapes=[pltpu.SemaphoreType.DMA((2,))],
        name="store",
    )(*results)


def solution(mesh):
    both = ("team", "loop")
    columns, rows = P(None, both), P(both)
    return jax.shard_map(
        shards,
        mesh=mesh,
        in_specs=(columns, columns, rows, columns, rows, rows, rows, columns),
        out_specs=(columns, P(None, both, None, None)),
        check_vma=False,
    )
```

```python
import functools
import math

import jax
import jax.numpy as jnp
from jax import lax
from jax.experimental import pallas as pl
from jax.experimental.pallas import tpu as pltpu
from jax.sharding import PartitionSpec as P

MESH = pl.DeviceIdType.MESH
F32, BF16 = jnp.float32, jnp.bfloat16
RING = 8
SRC = 512
ACT = 16
LANES = 128
TILE_W = 128


def split3(v):
    a = v.astype(BF16)
    r = v - a.astype(F32)
    b = r.astype(BF16)
    return a, b, (r - b.astype(F32)).astype(BF16)


def wide3(v):
    return [p.astype(F32) for p in split3(v)]


def wide2(v):
    a = v.astype(BF16).astype(F32)
    return a, (v - a).astype(BF16).astype(F32)


def coarse(v):
    return jnp.round(v * 32.0) * (1.0 / 32.0)


def pad_rows(v, rows):
    gap = jnp.zeros((rows - v.shape[0], v.shape[1]), v.dtype)
    return jnp.concatenate([v, gap], axis=0)


def features(pos, vel, soften):
    h, u = coarse(pos), coarse(vel)
    l, m = pos - h, vel - u
    l1, l2 = wide2(l)
    m1, m2 = wide2(m)
    total = lambda v: jnp.sum(v, axis=0, keepdims=True)
    hh = wide3(total(h * h))
    hl = wide3(total(2.0 * h * l + l * l) + (0.0 if soften is None else soften))
    hu = wide3(total(h * u))
    hm = wide3(total(h * m + l * u + l * m))
    ones = [jnp.ones_like(h)]
    if soften is None:
        near = [h] + hh + ones + [h, h, l1, l2, l1, l1, l2] + hl + ones
        dots = [h, u] + hu + ones + [h, h, m1, m2, l1, l2, u, u, l1, l1, l2, m1, m1, m2] + hm + ones
    else:
        near = [-2.0 * h] + ones + hh
        near += [-2.0 * l1, -2.0 * l2, -2.0 * h, -2.0 * h, -2.0 * l1, -2.0 * l2, -2.0 * l1] + ones + hl
        dots = [-u, -h] + ones + hu
        dots += [-m1, -m2, -h, -h, -u, -u, -l1, -l2, -m1, -m2, -m1, -l1, -l2, -l1] + ones + hm
    near = jnp.concatenate(near, axis=0)
    return near.shape[0], pad_rows(jnp.concatenate([near] + dots, axis=0), LANES)


def correct(targets, force, old_accel, level):
    step = jnp.exp2(-level)
    gap = old_accel[0:3] - force[0:3]
    first = -6.0 * gap - step * (4.0 * old_accel[3:6] + 2.0 * force[3:6])
    second = 12.0 * gap + 6.0 * step * (old_accel[3:6] + force[3:6])
    pos = targets[0:3] + step * step * (first / 24.0 + second / 120.0)
    vel = targets[3:6] + step * (first / 6.0 + second / 24.0)
    return jnp.concatenate([pos, vel, force], axis=0)

FOUR = 4
EARLY = 5


def kernel(
    gravity, soften,
    pos_in, vel_in, mass_in, old_in, index_in, level_in, tile_in, offset_in,
    state_ref, image_ref,
    pos_ref, vel_ref, mass_ref, old_ref, index_ref, level_ref, tile_ref, offset_ref,
    source, small, own, own_in, rest, rest_in, settled, targets, source_f, moments, near_f, dots_f,
    part, part_in, half, half_in, spread, gathered, tiles, tiles_all, left, right,
    load_sem, send_sem, recv_sem,
):
    team, loop = lax.axis_index("team"), lax.axis_index("loop")
    zh, y, c = team // 16, (team // 2) % 8, team % 2
    zl, x = loop // 4, loop % 4
    z = zh * 2 + zl

    def at(y, z, x, c):
        return ((z // 2) * 16 + y * 2 + c, (z % 2) * 4 + x)

    def step_of(s):
        away = (s + 1) // 2
        return away + (s + 1) % 2 * (8 - 2 * away)

    def y_peer(s, sign=1):
        return at((y + 8 + sign * step_of(s)) % 8, z, x, c)

    def z_peer(s):
        return at(y, (z + step_of(s)) % 8, x, c)

    def x_peer(s):
        return at(y, z, (x + s // 2) % 4, (c + s % 2) % 2)

    slots = range(1, RING)
    barrier = pltpu.get_barrier_semaphore()
    for s in reversed(slots):
        for peer in (y_peer(s), z_peer(s), x_peer(s)):
            pl.semaphore_signal(barrier, inc=1, device_id=peer, device_id_type=MESH)
    loads = [
        pltpu.make_async_copy(src, dst, load_sem.at[i])
        for i, (src, dst) in enumerate(
            (
                (pos_in, pos_ref), (vel_in, vel_ref), (mass_in, mass_ref), (index_in, index_ref),
                (old_in, old_ref), (level_in, level_ref), (tile_in, tile_ref), (offset_in, offset_ref),
            )
        )
    ]
    for one in loads:
        one.start()
    for one in loads:
        one.wait()

    def copy(stage, slot, src, dst, peer):
        return pltpu.make_async_remote_copy(
            src_ref=src,
            dst_ref=dst,
            send_sem=send_sem.at[stage],
            recv_sem=recv_sem.at[stage, slot],
            device_id=peer,
            device_id_type=MESH,
        )

    def await_all(stage, ref):
        copy(stage, 0, ref, ref, y_peer(1)).wait_recv()

    def await_sent(stage, ref):
        copy(stage, 0, ref, ref, y_peer(1)).wait_send()

    source[0, 0:3, :] = pos_ref[...]
    source[0, 3:6, :] = vel_ref[...]
    source[0, 6:7, :] = mass_ref[...].reshape(1, SRC)
    source[0, 7:8, :] = jnp.zeros((1, SRC), F32)
    small[...] = jnp.zeros_like(small)
    small[0:6, 0:ACT] = old_ref[...]
    small[6:7, 0:ACT] = level_ref[...].reshape(1, ACT).astype(F32)
    small[7:8, 0:ACT] = tile_ref[...].reshape(1, ACT).astype(F32)
    small[8:10, 0:ACT] = offset_ref[...].astype(F32)
    small[10:11, 0:ACT] = index_ref[...].reshape(1, ACT).astype(F32)
    place = x * 2 + c
    placed = pltpu.roll(small[...], place * ACT, 1)
    star = lax.broadcasted_iota(jnp.int32, (SRC, LANES), 0).astype(F32)
    lane = lax.broadcasted_iota(jnp.int32, (SRC, LANES), 1)
    chosen = jnp.where((star == placed[10:11]) & (lane // ACT == place), 1.0, 0.0).astype(BF16)
    pieces = jnp.concatenate(wide3(source[0]), axis=0).astype(BF16)
    picked = jnp.dot(pieces, chosen, preferred_element_type=F32)
    own[...] = picked[0:8] + picked[8:16] + picked[16:24]
    rest[...] = placed

    pl.semaphore_wait(barrier, 3 * (RING - 1))

    for s in (4, 5, 2, 3, 6, 7, 1):
        copy(0, 0, own, own_in.at[s - 1], x_peer(s)).start()
    for s in reversed(slots):
        copy(2, s, source.at[0], source.at[s], z_peer(s)).start()
    for s in slots:
        copy(1, 0, rest, rest_in.at[s - 1], x_peer(s)).start()

    def prepare_source(s):
        v = source[s]
        rows = slice(s * SRC, (s + 1) * SRC)
        source_f[rows, :] = jnp.transpose(features(v[0:3], v[3:6], None)[1]).astype(BF16)
        mass = v[6:7]
        sums = jnp.concatenate([v[0:3] * mass, v[3:6] * mass, mass, jnp.zeros_like(mass)], axis=0)
        moments[:, rows] = pad_rows(jnp.concatenate(wide3(sums), axis=0), 32).astype(BF16)

    def await_source(s):
        copy(2, s, source.at[0], source.at[s], z_peer(s)).wait_recv()

    def prepare_targets(first, last):
        t = jnp.concatenate([targets[s] for s in range(first, last)], axis=1)
        cut, f = features(t[0:3], t[3:6], soften)
        row = lax.broadcasted_iota(jnp.int32, f.shape, 0)
        lanes = slice(first * LANES, last * LANES)
        near_f[:, lanes] = jnp.where(row < cut, f, 0.0).astype(BF16)
        dots_f[:, lanes] = jnp.where(row < cut, 0.0, f).astype(BF16)

    def force_sums(s, first, last):
        lanes = pl.ds(pl.multiple_of(s * LANES, LANES), LANES)
        rows = slice(first * SRC, last * SRC)
        dist_sq = jnp.dot(source_f[rows, :], near_f[:, lanes], preferred_element_type=F32)
        dots = jnp.dot(source_f[rows, :], dots_f[:, lanes], preferred_element_type=F32)
        inverse = lax.rsqrt(dist_sq)
        inverse_sq = inverse * inverse
        strength = inverse * inverse_sq
        radial = (strength * inverse_sq) * dots
        plain = jnp.dot(moments[:, rows], strength.astype(BF16), preferred_element_type=F32)
        tilted = jnp.dot(moments[:, rows], radial.astype(BF16), preferred_element_type=F32)
        return plain[0:8] + plain[8:16] + plain[16:24], tilted[0:8] + tilted[8:16] + tilted[16:24]

    def combine(s, plain, tilted):
        t = targets[s]
        accel = plain[0:3] - t[0:3] * plain[6:7]
        jerk = (plain[3:6] - t[3:6] * plain[6:7]) - 3.0 * (tilted[0:3] - t[0:3] * tilted[6:7])
        part[s] = pad_rows(gravity * jnp.concatenate([accel, jerk], axis=0), 8)

    prepare_source(0)

    await_all(0, own_in)
    block = own[...]
    for s in slots:
        block = block + own_in[s - 1]
    targets[0] = block
    for s in reversed(slots):
        copy(3, s, targets.at[0], targets.at[s], y_peer(s)).start()
    prepare_targets(0, 1)
    for s in range(1, EARLY):
        await_source(s)
        prepare_source(s)
    plain, tilted = force_sums(0, 0, EARLY)

    await_all(1, rest_in)
    others = rest[...]
    for s in slots:
        others = others + rest_in[s - 1]
    settled[...] = others
    tiles[0] = others[7:8]
    for s in slots:
        copy(11, 0, tiles.at[0], tiles.at[s], z_peer(s)).start()
    image_ref[...] = jnp.zeros_like(image_ref)

    for s in range(EARLY, RING):
        await_source(s)
        prepare_source(s)
    more = force_sums(0, EARLY, RING)
    combine(0, plain + more[0], tilted + more[1])

    def await_targets(s):
        copy(3, s, targets.at[0], targets.at[s], y_peer(s)).wait_recv()

    def force_step(i, carry):
        @pl.when(i == 0)
        def _():
            await_targets(1)
            prepare_targets(1, 2)

        @pl.when(i == 1)
        def _():
            await_targets(3)
            prepare_targets(3, 4)

        @pl.when(i == 2)
        def _():
            for s in (2, 4, 5, 6, 7):
                await_targets(s)
            prepare_targets(4, RING)
            prepare_targets(2, 3)

        @pl.when(i == 3)
        def _():
            await_all(11, tiles.at[pl.ds(1, RING - 1)])
            for s in slots:
                copy(12, 0, tiles, tiles_all.at[s - 1], y_peer(s)).start()

        s = jnp.where(i < 2, 2 * i + 1, jnp.where(i == 2, 7, jnp.where(i == 3, 5, 14 - 2 * i)))
        combine(s, *force_sums(s, 0, RING))
        copy(4, s, part.at[s], part_in.at[s], y_peer(s, -1)).start()
        return carry

    lax.fori_loop(0, RING - 1, force_step, 0)

    total = part[0]
    for s in (1, 3, 7, 5, 6, 4, 2):
        copy(4, s, part.at[s], part_in.at[s], y_peer(s, -1)).wait_recv()
        total = total + part_in[s]
    half[...] = total
    for s in (4, 5, 2, 3, 6, 7, 1):
        copy(5, 0, half, half_in.at[s - 1], x_peer(s)).start()
    await_sent(0, own_in)
    await_sent(1, rest_in)
    await_sent(2, source.at[pl.ds(1, RING - 1)])
    await_sent(3, targets.at[pl.ds(1, RING - 1)])
    await_sent(4, part.at[pl.ds(1, RING - 1)])
    await_sent(11, tiles.at[pl.ds(1, RING - 1)])
    await_sent(12, tiles_all)
    await_all(12, tiles_all)
    await_all(5, half_in)
    for s in slots:
        total = total + half_in[s - 1]

    stars = targets[0]
    others = settled[...]
    state = correct(stars[0:6], total[0:6], others[0:6], others[6:7])
    centre_y = others[8:9] + (TILE_W / 16.0) * jnp.tanh(state[1:2])
    centre_x = others[9:10] + (TILE_W / 16.0) * jnp.tanh(state[0:1])
    mass = stars[6:7]
    spread[0] = jnp.concatenate([mass, mass * state[5:6] * state[5:6], centre_y, centre_x], axis=0)
    for s in reversed(slots):
        copy(6, s, spread.at[0], spread.at[s], z_peer(s)).start()

    def four(g, s, peer):
        piece = pl.ds(g * FOUR, FOUR)
        return copy(7 + g, s, spread.at[piece], gathered.at[s, piece], peer)

    mine = (team * 8 + loop).astype(F32)
    reach = (40.0 / TILE_W) * math.sqrt(0.5 * math.log2(math.e))
    cell = (lax.broadcasted_iota(jnp.int32, (TILE_W, LANES), 0).astype(F32) + 0.5) * reach

    def kernel_of(centre):
        scaled = cell - centre * reach
        return jnp.exp2(-(scaled * scaled))

    def add_stars(blocks):
        for b, (rows, tile) in enumerate(blocks):
            here = tile == mine
            rows_y, rows_x = kernel_of(rows[2:3]), kernel_of(rows[3:4])
            lanes = slice(b * LANES, (b + 1) * LANES)
            left[0:TILE_W, lanes] = (jnp.where(here, rows[0:1], 0.0) * rows_y).astype(BF16)
            left[TILE_W:, lanes] = (jnp.where(here, rows[1:2], 0.0) * rows_y).astype(BF16)
            right[:, lanes] = rows_x.astype(BF16)
        out = lax.dot_general(
            left[...], right[...], (((1,), (1,)), ((), ())), preferred_element_type=F32
        )
        image_ref[...] += out.reshape(2, 1, TILE_W, TILE_W)

    def forward(g):
        for s in range(max(1, g * FOUR), (g + 1) * FOUR):
            copy(6, s, spread.at[0], spread.at[s], z_peer(s)).wait_recv()
        for s in reversed(slots):
            four(g, s, y_peer(s)).start()
        add_stars([(spread[g * FOUR + k], tiles[g * FOUR + k]) for k in range(FOUR)])

    shifted = pltpu.roll(pad_rows(state, 16), (LANES - place * ACT) % LANES, 1)
    state_ref[...] = shifted[0:12, 0:ACT]
    forward(0)
    forward(1)

    def deposit_step(i, carry):
        g = jnp.where((i < 6) | (i == 8), 0, 1)
        s = jnp.where(i < 6, i + 1, jnp.where(i < 8, i - 5, jnp.where(i == 8, 7, i - 6)))
        four(g, s, y_peer(s)).wait_recv()
        add_stars([(gathered[s, g * FOUR + k], tiles_all[s - 1, g * FOUR + k]) for k in range(FOUR)])
        return carry

    lax.fori_loop(0, 2 * (RING - 1), deposit_step, 0)
    await_sent(5, half_in)
    await_sent(6, spread.at[pl.ds(1, RING - 1)])
    for g in range(RING // FOUR):
        await_sent(7 + g, gathered.at[pl.ds(1, RING - 1), pl.ds(g * FOUR, FOUR)])


def shards(*arrays):
    stars = SRC * RING**3
    stage_count = 13
    vmem = pl.BlockSpec(memory_space=pltpu.VMEM)
    outputs = (
        jax.ShapeDtypeStruct((12, ACT), F32),
        jax.ShapeDtypeStruct((2, 1, TILE_W, TILE_W), F32),
    )
    return pl.pallas_call(
        functools.partial(kernel, 1.0 / stars, float(stars) ** (-2.0 / 3.0)),
        out_shape=outputs,
        in_specs=[pl.BlockSpec(memory_space=pl.ANY)] * len(arrays),
        out_specs=(vmem, vmem),
        scratch_shapes=[pltpu.VMEM(v.shape, v.dtype) for v in arrays] + [
            pltpu.VMEM((RING, 8, SRC), F32),
            pltpu.VMEM((16, LANES), F32),
            pltpu.VMEM((8, LANES), F32),
            pltpu.VMEM((RING - 1, 8, LANES), F32),
            pltpu.VMEM((16, LANES), F32),
            pltpu.VMEM((RING - 1, 16, LANES), F32),
            pltpu.VMEM((16, LANES), F32),
            pltpu.VMEM((RING, 8, LANES), F32),
            pltpu.VMEM((RING * SRC, LANES), BF16),
            pltpu.VMEM((32, RING * SRC), BF16),
            pltpu.VMEM((LANES, RING * LANES), BF16),
            pltpu.VMEM((LANES, RING * LANES), BF16),
            pltpu.VMEM((RING, 8, LANES), F32),
            pltpu.VMEM((RING, 8, LANES), F32),
            pltpu.VMEM((8, LANES), F32),
            pltpu.VMEM((RING - 1, 8, LANES), F32),
            pltpu.VMEM((RING, 4, LANES), F32),
            pltpu.VMEM((RING, RING, 4, LANES), F32),
            pltpu.VMEM((RING, 1, LANES), F32),
            pltpu.VMEM((RING - 1, RING, 1, LANES), F32),
            pltpu.VMEM((2 * TILE_W, FOUR * LANES), BF16),
            pltpu.VMEM((TILE_W, FOUR * LANES), BF16),
            pltpu.SemaphoreType.DMA((len(arrays),)),
            pltpu.SemaphoreType.DMA((stage_count,)),
            pltpu.SemaphoreType.DMA((stage_count, RING)),
        ],
        compiler_params=pltpu.CompilerParams(
            collective_id=0, has_side_effects=True, vmem_limit_bytes=48 << 20
        ),
        name="cluster_step",
    )(*[pltpu.with_memory_space_constraint(v, pltpu.HBM) for v in arrays])


def solution(mesh):
    both = ("team", "loop")
    columns, rows = P(None, both), P(both)
    return jax.shard_map(
        shards,
        mesh=mesh,
        in_specs=(columns, columns, rows, columns, rows, rows, rows, columns),
        out_specs=(columns, P(None, both, None, None)),
        check_vma=False,
    )
```

```python
import functools
import math

import jax
import jax.numpy as jnp
from jax import lax
from jax.experimental import pallas as pl
from jax.experimental.pallas import tpu as pltpu
from jax.sharding import PartitionSpec as P

MESH = pl.DeviceIdType.MESH
F32, BF16 = jnp.float32, jnp.bfloat16
RING = 8
SRC = 512
ACT = 16
LANES = 128
TILE_W = 128


def split3(v):
    a = v.astype(BF16)
    r = v - a.astype(F32)
    b = r.astype(BF16)
    return a, b, (r - b.astype(F32)).astype(BF16)


def wide3(v):
    return [p.astype(F32) for p in split3(v)]


def wide2(v):
    a = v.astype(BF16).astype(F32)
    return a, (v - a).astype(BF16).astype(F32)


def coarse(v):
    return jnp.round(v * 32.0) * (1.0 / 32.0)


def pad_rows(v, rows):
    gap = jnp.zeros((rows - v.shape[0], v.shape[1]), v.dtype)
    return jnp.concatenate([v, gap], axis=0)


def features(pos, vel, soften):
    h, u = coarse(pos), coarse(vel)
    l, m = pos - h, vel - u
    l1, l2 = wide2(l)
    m1, m2 = wide2(m)
    total = lambda v: jnp.sum(v, axis=0, keepdims=True)
    hh = wide3(total(h * h))
    hl = wide3(total(2.0 * h * l + l * l) + (0.0 if soften is None else soften))
    hu = wide3(total(h * u))
    hm = wide3(total(h * m + l * u + l * m))
    ones = [jnp.ones_like(h)]
    if soften is None:
        near = [h] + hh + ones + [h, h, l1, l2, l1, l1, l2] + hl + ones
        dots = [h, u] + hu + ones + [h, h, m1, m2, l1, l2, u, u, l1, l1, l2, m1, m1, m2] + hm + ones
    else:
        near = [-2.0 * h] + ones + hh
        near += [-2.0 * l1, -2.0 * l2, -2.0 * h, -2.0 * h, -2.0 * l1, -2.0 * l2, -2.0 * l1] + ones + hl
        dots = [-u, -h] + ones + hu
        dots += [-m1, -m2, -h, -h, -u, -u, -l1, -l2, -m1, -m2, -m1, -l1, -l2, -l1] + ones + hm
    near = jnp.concatenate(near, axis=0)
    return near.shape[0], pad_rows(jnp.concatenate([near] + dots, axis=0), LANES)


def correct(targets, force, old_accel, level):
    step = jnp.exp2(-level)
    gap = old_accel[0:3] - force[0:3]
    first = -6.0 * gap - step * (4.0 * old_accel[3:6] + 2.0 * force[3:6])
    second = 12.0 * gap + 6.0 * step * (old_accel[3:6] + force[3:6])
    pos = targets[0:3] + step * step * (first / 24.0 + second / 120.0)
    vel = targets[3:6] + step * (first / 6.0 + second / 24.0)
    return jnp.concatenate([pos, vel, force], axis=0)

FOUR = 4
EARLY = 5


def kernel(
    gravity, soften,
    pos_in, vel_in, mass_in, old_in, index_in, level_in, tile_in, offset_in,
    state_ref, image_ref,
    pos_ref, vel_ref, mass_ref, old_ref, index_ref, level_ref, tile_ref, offset_ref,
    source, small, own, own_in, rest, rest_in, settled, targets, source_f, moments, near_f, dots_f,
    part, part_in, spread, gathered, tiles, tiles_all, left, right,
    load_sem, send_sem, recv_sem,
):
    team, loop = lax.axis_index("team"), lax.axis_index("loop")
    zh, y, c = team // 16, (team // 2) % 8, team % 2
    zl, x = loop // 4, loop % 4
    z = zh * 2 + zl

    def at(y, z, x, c):
        return ((z // 2) * 16 + y * 2 + c, (z % 2) * 4 + x)

    def step_of(s):
        away = (s + 1) // 2
        return away + (s + 1) % 2 * (8 - 2 * away)

    def y_peer(s, sign=1):
        return at((y + 8 + sign * step_of(s)) % 8, z, x, c)

    def z_peer(s):
        return at(y, (z + step_of(s)) % 8, x, c)

    def x_peer(s):
        return at(y, z, (x + s // 2) % 4, (c + s % 2) % 2)

    slots = range(1, RING)
    barrier = pltpu.get_barrier_semaphore()
    for s in reversed(slots):
        for peer in (y_peer(s), z_peer(s), x_peer(s)):
            pl.semaphore_signal(barrier, inc=1, device_id=peer, device_id_type=MESH)
    loads = [
        pltpu.make_async_copy(src, dst, load_sem.at[i])
        for i, (src, dst) in enumerate(
            (
                (pos_in, pos_ref), (vel_in, vel_ref), (mass_in, mass_ref), (index_in, index_ref),
                (old_in, old_ref), (level_in, level_ref), (tile_in, tile_ref), (offset_in, offset_ref),
            )
        )
    ]
    for one in loads:
        one.start()
    for one in loads:
        one.wait()

    def copy(stage, slot, src, dst, peer):
        return pltpu.make_async_remote_copy(
            src_ref=src,
            dst_ref=dst,
            send_sem=send_sem.at[stage],
            recv_sem=recv_sem.at[stage, slot],
            device_id=peer,
            device_id_type=MESH,
        )

    def await_all(stage, ref):
        copy(stage, 0, ref, ref, y_peer(1)).wait_recv()

    def await_sent(stage, ref):
        copy(stage, 0, ref, ref, y_peer(1)).wait_send()

    source[0, 0:3, :] = pos_ref[...]
    source[0, 3:6, :] = vel_ref[...]
    source[0, 6:7, :] = mass_ref[...].reshape(1, SRC)
    source[0, 7:8, :] = jnp.zeros((1, SRC), F32)
    small[...] = jnp.zeros_like(small)
    small[0:6, 0:ACT] = old_ref[...]
    small[6:7, 0:ACT] = level_ref[...].reshape(1, ACT).astype(F32)
    small[7:8, 0:ACT] = tile_ref[...].reshape(1, ACT).astype(F32)
    small[8:10, 0:ACT] = offset_ref[...].astype(F32)
    small[10:11, 0:ACT] = index_ref[...].reshape(1, ACT).astype(F32)
    place = x * 2 + c
    placed = pltpu.roll(small[...], place * ACT, 1)
    star = lax.broadcasted_iota(jnp.int32, (SRC, LANES), 0).astype(F32)
    lane = lax.broadcasted_iota(jnp.int32, (SRC, LANES), 1)
    chosen = jnp.where((star == placed[10:11]) & (lane // ACT == place), 1.0, 0.0).astype(BF16)
    pieces = jnp.concatenate(wide3(source[0]), axis=0).astype(BF16)
    picked = jnp.dot(pieces, chosen, preferred_element_type=F32)
    own[...] = picked[0:8] + picked[8:16] + picked[16:24]
    rest[...] = placed

    pl.semaphore_wait(barrier, 3 * (RING - 1))

    for s in (4, 5, 2, 3, 6, 7, 1):
        copy(0, 0, own, own_in.at[s - 1], x_peer(s)).start()
    for s in reversed(slots):
        copy(2, s, source.at[0], source.at[s], z_peer(s)).start()
    for s in slots:
        copy(1, 0, rest, rest_in.at[s - 1], x_peer(s)).start()

    def prepare_source(s):
        v = source[s]
        rows = slice(s * SRC, (s + 1) * SRC)
        source_f[rows, :] = jnp.transpose(features(v[0:3], v[3:6], None)[1]).astype(BF16)
        mass = v[6:7]
        sums = jnp.concatenate([v[0:3] * mass, v[3:6] * mass, mass, jnp.zeros_like(mass)], axis=0)
        moments[:, rows] = pad_rows(jnp.concatenate(wide3(sums), axis=0), 32).astype(BF16)

    def await_source(s):
        copy(2, s, source.at[0], source.at[s], z_peer(s)).wait_recv()

    def prepare_targets(first, last):
        t = jnp.concatenate([targets[s] for s in range(first, last)], axis=1)
        cut, f = features(t[0:3], t[3:6], soften)
        row = lax.broadcasted_iota(jnp.int32, f.shape, 0)
        lanes = slice(first * LANES, last * LANES)
        near_f[:, lanes] = jnp.where(row < cut, f, 0.0).astype(BF16)
        dots_f[:, lanes] = jnp.where(row < cut, 0.0, f).astype(BF16)

    def force_sums(s, first, last):
        lanes = pl.ds(pl.multiple_of(s * LANES, LANES), LANES)
        rows = slice(first * SRC, last * SRC)
        dist_sq = jnp.dot(source_f[rows, :], near_f[:, lanes], preferred_element_type=F32)
        dots = jnp.dot(source_f[rows, :], dots_f[:, lanes], preferred_element_type=F32)
        inverse = lax.rsqrt(dist_sq)
        inverse_sq = inverse * inverse
        strength = inverse * inverse_sq
        radial = (strength * inverse_sq) * dots
        plain = jnp.dot(moments[:, rows], strength.astype(BF16), preferred_element_type=F32)
        tilted = jnp.dot(moments[:, rows], radial.astype(BF16), preferred_element_type=F32)
        return plain[0:8] + plain[8:16] + plain[16:24], tilted[0:8] + tilted[8:16] + tilted[16:24]

    def combine(s, plain, tilted):
        t = targets[s]
        accel = plain[0:3] - t[0:3] * plain[6:7]
        jerk = (plain[3:6] - t[3:6] * plain[6:7]) - 3.0 * (tilted[0:3] - t[0:3] * tilted[6:7])
        part[s] = pad_rows(gravity * jnp.concatenate([accel, jerk], axis=0), 8)

    prepare_source(0)

    await_all(0, own_in)
    block = own[...]
    for s in slots:
        block = block + own_in[s - 1]
    targets[0] = block
    for s in reversed(slots):
        copy(3, s, targets.at[0], targets.at[s], y_peer(s)).start()
    prepare_targets(0, 1)
    for s in range(1, EARLY):
        await_source(s)
        prepare_source(s)
    plain, tilted = force_sums(0, 0, EARLY)

    await_all(1, rest_in)
    others = rest[...]
    for s in slots:
        others = others + rest_in[s - 1]
    settled[...] = others
    tiles[0] = others[7:8]
    for s in slots:
        copy(11, 0, tiles.at[0], tiles.at[s], z_peer(s)).start()
    image_ref[...] = jnp.zeros_like(image_ref)

    for s in range(EARLY, RING):
        await_source(s)
        prepare_source(s)
    more = force_sums(0, EARLY, RING)
    combine(0, plain + more[0], tilted + more[1])

    def await_targets(s):
        copy(3, s, targets.at[0], targets.at[s], y_peer(s)).wait_recv()

    def give(s, first):
        back = (y + 8 - step_of(s)) % 8
        for q in (4, 5, 2, 3, 6, 7, 1, 0):
            if q >= first:
                peer = at(back, z, (x + q // 2) % 4, (c + q % 2) % 2)
                copy(4, 0, part.at[s], part_in.at[s * RING + q], peer).start()

    give(0, 1)

    def force_step(i, carry):
        @pl.when(i == 0)
        def _():
            await_targets(1)
            prepare_targets(1, 2)

        @pl.when(i == 1)
        def _():
            await_targets(3)
            prepare_targets(3, 4)

        @pl.when(i == 2)
        def _():
            for s in (2, 4, 5, 6, 7):
                await_targets(s)
            prepare_targets(4, RING)
            prepare_targets(2, 3)

        @pl.when(i == 3)
        def _():
            await_all(11, tiles.at[pl.ds(1, RING - 1)])
            for s in slots:
                copy(12, 0, tiles, tiles_all.at[s - 1], y_peer(s)).start()

        s = jnp.where(i < 2, 2 * i + 1, jnp.where(i == 2, 7, jnp.where(i == 3, 5, 14 - 2 * i)))
        combine(s, *force_sums(s, 0, RING))
        give(s, 0)
        return carry

    lax.fori_loop(0, RING - 1, force_step, 0)

    await_sent(0, own_in)
    await_sent(1, rest_in)
    await_sent(2, source.at[pl.ds(1, RING - 1)])
    await_sent(3, targets.at[pl.ds(1, RING - 1)])
    await_sent(11, tiles.at[pl.ds(1, RING - 1)])
    await_sent(12, tiles_all)
    await_all(12, tiles_all)
    await_all(4, part_in.at[pl.ds(1, RING * RING - 1)])
    total = part[0] + jnp.sum(part_in[1:], axis=0)

    stars = targets[0]
    others = settled[...]
    state = correct(stars[0:6], total[0:6], others[0:6], others[6:7])
    centre_y = others[8:9] + (TILE_W / 16.0) * jnp.tanh(state[1:2])
    centre_x = others[9:10] + (TILE_W / 16.0) * jnp.tanh(state[0:1])
    mass = stars[6:7]
    spread[0] = jnp.concatenate([mass, mass * state[5:6] * state[5:6], centre_y, centre_x], axis=0)
    for s in reversed(slots):
        copy(6, s, spread.at[0], spread.at[s], z_peer(s)).start()

    def four(g, s, peer):
        piece = pl.ds(g * FOUR, FOUR)
        return copy(7 + g, s, spread.at[piece], gathered.at[s, piece], peer)

    mine = (team * 8 + loop).astype(F32)
    reach = (40.0 / TILE_W) * math.sqrt(0.5 * math.log2(math.e))
    cell = (lax.broadcasted_iota(jnp.int32, (TILE_W, LANES), 0).astype(F32) + 0.5) * reach

    def kernel_of(centre):
        scaled = cell - centre * reach
        return jnp.exp2(-(scaled * scaled))

    def build(half, blocks):
        for b, (rows, tile) in enumerate(blocks):
            here = tile == mine
            rows_y, rows_x = kernel_of(rows[2:3]), kernel_of(rows[3:4])
            lanes = slice((half * FOUR + b) * LANES, (half * FOUR + b + 1) * LANES)
            left[0:TILE_W, lanes] = (jnp.where(here, rows[0:1], 0.0) * rows_y).astype(BF16)
            left[TILE_W:, lanes] = (jnp.where(here, rows[1:2], 0.0) * rows_y).astype(BF16)
            right[:, lanes] = rows_x.astype(BF16)

    def add_stars():
        out = lax.dot_general(
            left[...], right[...], (((1,), (1,)), ((), ())), preferred_element_type=F32
        )
        image_ref[...] += out.reshape(2, 1, TILE_W, TILE_W)

    def forward(g):
        for s in range(max(1, g * FOUR), (g + 1) * FOUR):
            copy(6, s, spread.at[0], spread.at[s], z_peer(s)).wait_recv()
        for s in reversed(slots):
            four(g, s, y_peer(s)).start()
        build(g, [(spread[g * FOUR + k], tiles[g * FOUR + k]) for k in range(FOUR)])

    shifted = pltpu.roll(pad_rows(state, 16), (LANES - place * ACT) % LANES, 1)
    state_ref[...] = shifted[0:12, 0:ACT]
    forward(0)
    forward(1)
    add_stars()

    def deposit_step(j, carry):
        for half in (0, 1):
            i = 2 * j + half
            g = jnp.where((i < 6) | (i == 8), 0, 1)
            s = jnp.where(i < 6, i + 1, jnp.where(i < 8, i - 5, jnp.where(i == 8, 7, i - 6)))
            four(g, s, y_peer(s)).wait_recv()
            build(half, [(gathered[s, g * FOUR + k], tiles_all[s - 1, g * FOUR + k]) for k in range(FOUR)])
        add_stars()
        return carry

    lax.fori_loop(0, RING - 1, deposit_step, 0)
    await_sent(4, part_in.at[pl.ds(1, RING * RING - 1)])
    await_sent(6, spread.at[pl.ds(1, RING - 1)])
    for g in range(RING // FOUR):
        await_sent(7 + g, gathered.at[pl.ds(1, RING - 1), pl.ds(g * FOUR, FOUR)])


def shards(*arrays):
    stars = SRC * RING**3
    stage_count = 13
    vmem = pl.BlockSpec(memory_space=pltpu.VMEM)
    outputs = (
        jax.ShapeDtypeStruct((12, ACT), F32),
        jax.ShapeDtypeStruct((2, 1, TILE_W, TILE_W), F32),
    )
    return pl.pallas_call(
        functools.partial(kernel, 1.0 / stars, float(stars) ** (-2.0 / 3.0)),
        out_shape=outputs,
        in_specs=[pl.BlockSpec(memory_space=pl.ANY)] * len(arrays),
        out_specs=(vmem, vmem),
        scratch_shapes=[pltpu.VMEM(v.shape, v.dtype) for v in arrays] + [
            pltpu.VMEM((RING, 8, SRC), F32),
            pltpu.VMEM((16, LANES), F32),
            pltpu.VMEM((8, LANES), F32),
            pltpu.VMEM((RING - 1, 8, LANES), F32),
            pltpu.VMEM((16, LANES), F32),
            pltpu.VMEM((RING - 1, 16, LANES), F32),
            pltpu.VMEM((16, LANES), F32),
            pltpu.VMEM((RING, 8, LANES), F32),
            pltpu.VMEM((RING * SRC, LANES), BF16),
            pltpu.VMEM((32, RING * SRC), BF16),
            pltpu.VMEM((LANES, RING * LANES), BF16),
            pltpu.VMEM((LANES, RING * LANES), BF16),
            pltpu.VMEM((RING, 8, LANES), F32),
            pltpu.VMEM((RING * RING, 8, LANES), F32),
            pltpu.VMEM((RING, 4, LANES), F32),
            pltpu.VMEM((RING, RING, 4, LANES), F32),
            pltpu.VMEM((RING, 1, LANES), F32),
            pltpu.VMEM((RING - 1, RING, 1, LANES), F32),
            pltpu.VMEM((2 * TILE_W, 2 * FOUR * LANES), BF16),
            pltpu.VMEM((TILE_W, 2 * FOUR * LANES), BF16),
            pltpu.SemaphoreType.DMA((len(arrays),)),
            pltpu.SemaphoreType.DMA((stage_count,)),
            pltpu.SemaphoreType.DMA((stage_count, RING)),
        ],
        compiler_params=pltpu.CompilerParams(
            collective_id=0, has_side_effects=True, vmem_limit_bytes=48 << 20
        ),
        name="cluster_step",
    )(*[pltpu.with_memory_space_constraint(v, pltpu.HBM) for v in arrays])


def solution(mesh):
    both = ("team", "loop")
    columns, rows = P(None, both), P(both)
    return jax.shard_map(
        shards,
        mesh=mesh,
        in_specs=(columns, columns, rows, columns, rows, rows, rows, columns),
        out_specs=(columns, P(None, both, None, None)),
        check_vma=False,
    )
```

```python
import functools
import math

import jax
import jax.numpy as jnp
from jax import lax
from jax.experimental import pallas as pl
from jax.experimental.pallas import tpu as pltpu
from jax.sharding import PartitionSpec as P

MESH = pl.DeviceIdType.MESH
F32, BF16 = jnp.float32, jnp.bfloat16
RING = 8
SRC = 512
ACT = 16
LANES = 128
TILE_W = 128


def split3(v):
    a = v.astype(BF16)
    r = v - a.astype(F32)
    b = r.astype(BF16)
    return a, b, (r - b.astype(F32)).astype(BF16)


def wide3(v):
    return [p.astype(F32) for p in split3(v)]


def wide2(v):
    a = v.astype(BF16).astype(F32)
    return a, (v - a).astype(BF16).astype(F32)


def coarse(v):
    return jnp.round(v * 32.0) * (1.0 / 32.0)


def pad_rows(v, rows):
    gap = jnp.zeros((rows - v.shape[0], v.shape[1]), v.dtype)
    return jnp.concatenate([v, gap], axis=0)


def features(pos, vel, soften):
    h, u = coarse(pos), coarse(vel)
    l, m = pos - h, vel - u
    l1, l2 = wide2(l)
    m1, m2 = wide2(m)
    total = lambda v: jnp.sum(v, axis=0, keepdims=True)
    hh = wide3(total(h * h))
    hl = wide3(total(2.0 * h * l + l * l) + (0.0 if soften is None else soften))
    hu = wide3(total(h * u))
    hm = wide3(total(h * m + l * u + l * m))
    ones = [jnp.ones_like(h)]
    if soften is None:
        near = [h] + hh + ones + [h, h, l1, l2, l1, l1, l2] + hl + ones
        dots = [h, u] + hu + ones + [h, h, m1, m2, l1, l2, u, u, l1, l1, l2, m1, m1, m2] + hm + ones
    else:
        near = [-2.0 * h] + ones + hh
        near += [-2.0 * l1, -2.0 * l2, -2.0 * h, -2.0 * h, -2.0 * l1, -2.0 * l2, -2.0 * l1] + ones + hl
        dots = [-u, -h] + ones + hu
        dots += [-m1, -m2, -h, -h, -u, -u, -l1, -l2, -m1, -m2, -m1, -l1, -l2, -l1] + ones + hm
    near = jnp.concatenate(near, axis=0)
    return near.shape[0], pad_rows(jnp.concatenate([near] + dots, axis=0), LANES)


def correct(targets, force, old_accel, level):
    step = jnp.exp2(-level)
    gap = old_accel[0:3] - force[0:3]
    first = -6.0 * gap - step * (4.0 * old_accel[3:6] + 2.0 * force[3:6])
    second = 12.0 * gap + 6.0 * step * (old_accel[3:6] + force[3:6])
    pos = targets[0:3] + step * step * (first / 24.0 + second / 120.0)
    vel = targets[3:6] + step * (first / 6.0 + second / 24.0)
    return jnp.concatenate([pos, vel, force], axis=0)

FOUR = 4
ORDER = sorted(
    ((a, b) for a in range(RING) for b in range(RING)), key=lambda p: ((p[0] + 1) // 2 + (p[1] + 1) // 2, p)
)
EARLY = 5


def kernel(
    gravity, soften,
    pos_in, vel_in, mass_in, old_in, index_in, level_in, tile_in, offset_in,
    state_ref, image_ref,
    pos_ref, vel_ref, mass_ref, old_ref, index_ref, level_ref, tile_ref, offset_ref,
    source, small, own, own_in, rest, rest_in, settled, targets, source_f, moments, near_f, dots_f,
    part, part_in, spread, gathered, tiles, tiles_in, tiles_all, left, right,
    load_sem, send_sem, recv_sem, deposit_sem,
):
    team, loop = lax.axis_index("team"), lax.axis_index("loop")
    zh, y, c = team // 16, (team // 2) % 8, team % 2
    zl, x = loop // 4, loop % 4
    z = zh * 2 + zl

    def at(y, z, x, c):
        return ((z // 2) * 16 + y * 2 + c, (z % 2) * 4 + x)

    def step_of(s):
        away = (s + 1) // 2
        return away + (s + 1) % 2 * (8 - 2 * away)

    def y_peer(s, sign=1):
        return at((y + 8 + sign * step_of(s)) % 8, z, x, c)

    def z_peer(s):
        return at(y, (z + step_of(s)) % 8, x, c)

    def x_peer(s):
        return at(y, z, (x + s // 2) % 4, (c + s % 2) % 2)

    slots = range(1, RING)
    barrier = pltpu.get_barrier_semaphore()
    for s in reversed(slots):
        for peer in (y_peer(s), z_peer(s), x_peer(s)):
            pl.semaphore_signal(barrier, inc=1, device_id=peer, device_id_type=MESH)
    loads = [
        pltpu.make_async_copy(src, dst, load_sem.at[i])
        for i, (src, dst) in enumerate(
            (
                (pos_in, pos_ref), (vel_in, vel_ref), (mass_in, mass_ref), (index_in, index_ref),
                (old_in, old_ref), (level_in, level_ref), (tile_in, tile_ref), (offset_in, offset_ref),
            )
        )
    ]
    for one in loads:
        one.start()
    for one in loads:
        one.wait()

    def copy(stage, slot, src, dst, peer):
        return pltpu.make_async_remote_copy(
            src_ref=src,
            dst_ref=dst,
            send_sem=send_sem.at[stage],
            recv_sem=recv_sem.at[stage, slot],
            device_id=peer,
            device_id_type=MESH,
        )

    def await_all(stage, ref):
        copy(stage, 0, ref, ref, y_peer(1)).wait_recv()

    def await_sent(stage, ref):
        copy(stage, 0, ref, ref, y_peer(1)).wait_send()

    source[0, 0:3, :] = pos_ref[...]
    source[0, 3:6, :] = vel_ref[...]
    source[0, 6:7, :] = mass_ref[...].reshape(1, SRC)
    source[0, 7:8, :] = jnp.zeros((1, SRC), F32)
    small[...] = jnp.zeros_like(small)
    small[0:6, 0:ACT] = old_ref[...]
    small[6:7, 0:ACT] = level_ref[...].reshape(1, ACT).astype(F32)
    small[7:8, 0:ACT] = tile_ref[...].reshape(1, ACT).astype(F32)
    small[8:10, 0:ACT] = offset_ref[...].astype(F32)
    small[10:11, 0:ACT] = index_ref[...].reshape(1, ACT).astype(F32)
    place = x * 2 + c
    placed = pltpu.roll(small[...], place * ACT, 1)
    star = lax.broadcasted_iota(jnp.int32, (SRC, LANES), 0).astype(F32)
    lane = lax.broadcasted_iota(jnp.int32, (SRC, LANES), 1)
    chosen = jnp.where((star == placed[10:11]) & (lane // ACT == place), 1.0, 0.0).astype(BF16)
    pieces = jnp.concatenate(wide3(source[0]), axis=0).astype(BF16)
    picked = jnp.dot(pieces, chosen, preferred_element_type=F32)
    own[...] = picked[0:8] + picked[8:16] + picked[16:24]
    rest[...] = placed

    pl.semaphore_wait(barrier, 3 * (RING - 1))

    for s in reversed(slots):
        copy(2, s, source.at[0], source.at[s], z_peer(s)).start()
    for s in (4, 5, 2, 3, 6, 7, 1):
        copy(0, 0, own, own_in.at[s - 1], x_peer(s)).start()
    for s in slots:
        copy(1, 0, rest, rest_in.at[s - 1], x_peer(s)).start()

    def prepare_source(s):
        v = source[s]
        rows = slice(s * SRC, (s + 1) * SRC)
        source_f[rows, :] = jnp.transpose(features(v[0:3], v[3:6], None)[1]).astype(BF16)
        mass = v[6:7]
        sums = jnp.concatenate([v[0:3] * mass, v[3:6] * mass, mass, jnp.zeros_like(mass)], axis=0)
        moments[:, rows] = pad_rows(jnp.concatenate(wide3(sums), axis=0), 32).astype(BF16)

    def await_source(s):
        copy(2, s, source.at[0], source.at[s], z_peer(s)).wait_recv()

    def prepare_targets(first, last):
        t = jnp.concatenate([targets[s] for s in range(first, last)], axis=1)
        cut, f = features(t[0:3], t[3:6], soften)
        row = lax.broadcasted_iota(jnp.int32, f.shape, 0)
        lanes = slice(first * LANES, last * LANES)
        near_f[:, lanes] = jnp.where(row < cut, f, 0.0).astype(BF16)
        dots_f[:, lanes] = jnp.where(row < cut, 0.0, f).astype(BF16)

    def force_sums(s, first, last):
        lanes = pl.ds(pl.multiple_of(s * LANES, LANES), LANES)
        rows = slice(first * SRC, last * SRC)
        dist_sq = jnp.dot(source_f[rows, :], near_f[:, lanes], preferred_element_type=F32)
        dots = jnp.dot(source_f[rows, :], dots_f[:, lanes], preferred_element_type=F32)
        inverse = lax.rsqrt(dist_sq)
        inverse_sq = inverse * inverse
        strength = inverse * inverse_sq
        radial = (strength * inverse_sq) * dots
        plain = jnp.dot(moments[:, rows], strength.astype(BF16), preferred_element_type=F32)
        tilted = jnp.dot(moments[:, rows], radial.astype(BF16), preferred_element_type=F32)
        return plain[0:8] + plain[8:16] + plain[16:24], tilted[0:8] + tilted[8:16] + tilted[16:24]

    def combine(s, plain, tilted):
        t = targets[s]
        accel = plain[0:3] - t[0:3] * plain[6:7]
        jerk = (plain[3:6] - t[3:6] * plain[6:7]) - 3.0 * (tilted[0:3] - t[0:3] * tilted[6:7])
        part[s] = pad_rows(gravity * jnp.concatenate([accel, jerk], axis=0), 8)

    prepare_source(0)

    await_all(0, own_in)
    block = own[...]
    for s in slots:
        block = block + own_in[s - 1]
    targets[0] = block
    for s in reversed(slots):
        copy(3, s, targets.at[0], targets.at[s], y_peer(s)).start()
    prepare_targets(0, 1)
    for s in range(1, EARLY):
        await_source(s)
        prepare_source(s)
    plain, tilted = force_sums(0, 0, EARLY)

    await_all(1, rest_in)
    others = rest[...]
    for s in slots:
        others = others + rest_in[s - 1]
    settled[...] = others
    tiles[0] = others[7:8]
    for s in slots:
        copy(11, 0, tiles.at[0], tiles.at[s], z_peer(s)).start()
    image_ref[...] = jnp.zeros_like(image_ref)

    for s in range(EARLY, RING):
        await_source(s)
        prepare_source(s)
    more = force_sums(0, EARLY, RING)
    combine(0, plain + more[0], tilted + more[1])

    def await_targets(s):
        copy(3, s, targets.at[0], targets.at[s], y_peer(s)).wait_recv()

    def give(s, first):
        back = (y + 8 - step_of(s)) % 8
        for q in (4, 5, 2, 3, 6, 7, 1, 0):
            if q >= first:
                peer = at(back, z, (x + q // 2) % 4, (c + q % 2) % 2)
                copy(4, 0, part.at[s], part_in.at[s * RING + q], peer).start()

    give(0, 1)

    def force_step(i, carry):
        @pl.when(i == 0)
        def _():
            await_targets(1)
            prepare_targets(1, 2)

        @pl.when(i == 1)
        def _():
            await_targets(3)
            prepare_targets(3, 4)

        @pl.when(i == 2)
        def _():
            for s in (2, 4, 5, 6, 7):
                await_targets(s)
            prepare_targets(4, RING)
            prepare_targets(2, 3)

        @pl.when(i == 3)
        def _():
            await_all(11, tiles.at[pl.ds(1, RING - 1)])
            for s in slots:
                copy(12, 0, tiles, tiles_in.at[s - 1], y_peer(s)).start()

        s = jnp.where(i < 2, 2 * i + 1, jnp.where(i == 2, 7, jnp.where(i == 3, 5, 14 - 2 * i)))
        combine(s, *force_sums(s, 0, RING))
        give(s, 0)
        return carry

    lax.fori_loop(0, RING - 1, force_step, 0)

    await_sent(0, own_in)
    await_sent(1, rest_in)
    await_sent(2, source.at[pl.ds(1, RING - 1)])
    await_sent(3, targets.at[pl.ds(1, RING - 1)])
    await_sent(11, tiles.at[pl.ds(1, RING - 1)])
    await_sent(12, tiles_in)
    await_all(12, tiles_in)
    for i, (away_y, away_z) in enumerate(ORDER):
        tiles_all[i] = tiles_in[away_y - 1, away_z] if away_y else tiles[away_z]
    await_all(4, part_in.at[pl.ds(1, RING * RING - 1)])
    total = part[0] + jnp.sum(part_in[1:], axis=0)

    stars = targets[0]
    others = settled[...]
    state = correct(stars[0:6], total[0:6], others[0:6], others[6:7])
    centre_y = others[8:9] + (TILE_W / 16.0) * jnp.tanh(state[1:2])
    centre_x = others[9:10] + (TILE_W / 16.0) * jnp.tanh(state[0:1])
    mass = stars[6:7]
    spread[...] = jnp.concatenate([mass, mass * state[5:6] * state[5:6], centre_y, centre_x], axis=0)
    gathered[0] = spread[...]

    def deposit(i):
        away_y, away_z = ORDER[i]
        return pltpu.make_async_remote_copy(
            src_ref=spread,
            dst_ref=gathered.at[i],
            send_sem=send_sem.at[6],
            recv_sem=deposit_sem.at[i // FOUR],
            device_id=at((y + step_of(away_y)) % 8, (z + step_of(away_z)) % 8, x, c),
            device_id_type=MESH,
        )

    for i in range(1, len(ORDER)):
        deposit(i).start()

    def await_deposits(first, count):
        these = gathered.at[pl.ds(first, count)]
        pltpu.make_async_remote_copy(
            src_ref=these,
            dst_ref=these,
            send_sem=send_sem.at[6],
            recv_sem=deposit_sem.at[first // FOUR],
            device_id=y_peer(1),
            device_id_type=MESH,
        ).wait_recv()

    mine = (team * 8 + loop).astype(F32)
    reach = (40.0 / TILE_W) * math.sqrt(0.5 * math.log2(math.e))
    cell = (lax.broadcasted_iota(jnp.int32, (TILE_W, LANES), 0).astype(F32) + 0.5) * reach

    def kernel_of(centre):
        scaled = cell - centre * reach
        return jnp.exp2(-(scaled * scaled))

    def build(half, blocks):
        for b, (rows, tile) in enumerate(blocks):
            here = tile == mine
            rows_y, rows_x = kernel_of(rows[2:3]), kernel_of(rows[3:4])
            lanes = slice((half * FOUR + b) * LANES, (half * FOUR + b + 1) * LANES)
            left[0:TILE_W, lanes] = (jnp.where(here, rows[0:1], 0.0) * rows_y).astype(BF16)
            left[TILE_W:, lanes] = (jnp.where(here, rows[1:2], 0.0) * rows_y).astype(BF16)
            right[:, lanes] = rows_x.astype(BF16)

    def add_stars():
        out = lax.dot_general(
            left[...], right[...], (((1,), (1,)), ((), ())), preferred_element_type=F32
        )
        image_ref[...] += out.reshape(2, 1, TILE_W, TILE_W)

    shifted = pltpu.roll(pad_rows(state, 16), (LANES - place * ACT) % LANES, 1)
    state_ref[...] = shifted[0:12, 0:ACT]

    def build_four(half, first):
        build(half, [(gathered[first + k], tiles_all[first + k]) for k in range(FOUR)])

    await_deposits(1, FOUR - 1)
    build_four(0, 0)
    await_deposits(FOUR, FOUR)
    build_four(1, FOUR)
    add_stars()

    def deposit_step(j, carry):
        for half in (0, 1):
            first = (2 * j + half) * FOUR
            await_deposits(first, FOUR)
            build_four(half, first)
        add_stars()
        return carry

    lax.fori_loop(1, RING, deposit_step, 0)
    await_sent(4, part_in.at[pl.ds(1, RING * RING - 1)])
    await_sent(6, gathered.at[pl.ds(1, len(ORDER) - 1)])


def shards(*arrays):
    stars = SRC * RING**3
    stage_count = 13
    vmem = pl.BlockSpec(memory_space=pltpu.VMEM)
    outputs = (
        jax.ShapeDtypeStruct((12, ACT), F32),
        jax.ShapeDtypeStruct((2, 1, TILE_W, TILE_W), F32),
    )
    return pl.pallas_call(
        functools.partial(kernel, 1.0 / stars, float(stars) ** (-2.0 / 3.0)),
        out_shape=outputs,
        in_specs=[pl.BlockSpec(memory_space=pl.ANY)] * len(arrays),
        out_specs=(vmem, vmem),
        scratch_shapes=[pltpu.VMEM(v.shape, v.dtype) for v in arrays] + [
            pltpu.VMEM((RING, 8, SRC), F32),
            pltpu.VMEM((16, LANES), F32),
            pltpu.VMEM((8, LANES), F32),
            pltpu.VMEM((RING - 1, 8, LANES), F32),
            pltpu.VMEM((16, LANES), F32),
            pltpu.VMEM((RING - 1, 16, LANES), F32),
            pltpu.VMEM((16, LANES), F32),
            pltpu.VMEM((RING, 8, LANES), F32),
            pltpu.VMEM((RING * SRC, LANES), BF16),
            pltpu.VMEM((32, RING * SRC), BF16),
            pltpu.VMEM((LANES, RING * LANES), BF16),
            pltpu.VMEM((LANES, RING * LANES), BF16),
            pltpu.VMEM((RING, 8, LANES), F32),
            pltpu.VMEM((RING * RING, 8, LANES), F32),
            pltpu.VMEM((4, LANES), F32),
            pltpu.VMEM((RING * RING, 4, LANES), F32),
            pltpu.VMEM((RING, 1, LANES), F32),
            pltpu.VMEM((RING - 1, RING, 1, LANES), F32),
            pltpu.VMEM((RING * RING, 1, LANES), F32),
            pltpu.VMEM((2 * TILE_W, 2 * FOUR * LANES), BF16),
            pltpu.VMEM((TILE_W, 2 * FOUR * LANES), BF16),
            pltpu.SemaphoreType.DMA((len(arrays),)),
            pltpu.SemaphoreType.DMA((stage_count,)),
            pltpu.SemaphoreType.DMA((stage_count, RING)),
            pltpu.SemaphoreType.DMA((RING * RING // FOUR,)),
        ],
        compiler_params=pltpu.CompilerParams(
            collective_id=0, has_side_effects=True, vmem_limit_bytes=48 << 20
        ),
        name="cluster_step",
    )(*[pltpu.with_memory_space_constraint(v, pltpu.HBM) for v in arrays])


def solution(mesh):
    both = ("team", "loop")
    columns, rows = P(None, both), P(both)
    return jax.shard_map(
        shards,
        mesh=mesh,
        in_specs=(columns, columns, rows, columns, rows, rows, rows, columns),
        out_specs=(columns, P(None, both, None, None)),
        check_vma=False,
    )
```

```python
import functools
import math

import jax
import jax.numpy as jnp
from jax import lax
from jax.experimental import pallas as pl
from jax.experimental.pallas import tpu as pltpu
from jax.sharding import PartitionSpec as P

MESH = pl.DeviceIdType.MESH
F32, BF16 = jnp.float32, jnp.bfloat16
RING = 8
SRC = 512
ACT = 16
LANES = 128
TILE_W = 128


def split3(v):
    a = v.astype(BF16)
    r = v - a.astype(F32)
    b = r.astype(BF16)
    return a, b, (r - b.astype(F32)).astype(BF16)


def wide3(v):
    return [p.astype(F32) for p in split3(v)]


def wide2(v):
    a = v.astype(BF16).astype(F32)
    return a, (v - a).astype(BF16).astype(F32)


def coarse(v):
    return jnp.round(v * 32.0) * (1.0 / 32.0)


def pad_rows(v, rows):
    gap = jnp.zeros((rows - v.shape[0], v.shape[1]), v.dtype)
    return jnp.concatenate([v, gap], axis=0)


def features(pos, vel, soften):
    h, u = coarse(pos), coarse(vel)
    l, m = pos - h, vel - u
    l1, l2 = wide2(l)
    m1, m2 = wide2(m)
    total = lambda v: jnp.sum(v, axis=0, keepdims=True)
    hh = wide3(total(h * h))
    hl = wide3(total(2.0 * h * l + l * l) + (0.0 if soften is None else soften))
    hu = wide3(total(h * u))
    hm = wide3(total(h * m + l * u + l * m))
    ones = [jnp.ones_like(h)]
    if soften is None:
        near = [h] + hh + ones + [h, h, l1, l2, l1, l1, l2] + hl + ones
        dots = [h, u] + hu + ones + [h, h, m1, m2, l1, l2, u, u, l1, l1, l2, m1, m1, m2] + hm + ones
    else:
        near = [-2.0 * h] + ones + hh
        near += [-2.0 * l1, -2.0 * l2, -2.0 * h, -2.0 * h, -2.0 * l1, -2.0 * l2, -2.0 * l1] + ones + hl
        dots = [-u, -h] + ones + hu
        dots += [-m1, -m2, -h, -h, -u, -u, -l1, -l2, -m1, -m2, -m1, -l1, -l2, -l1] + ones + hm
    near = jnp.concatenate(near, axis=0)
    return near.shape[0], pad_rows(jnp.concatenate([near] + dots, axis=0), LANES)


def correct(targets, force, old_accel, level):
    step = jnp.exp2(-level)
    gap = old_accel[0:3] - force[0:3]
    first = -6.0 * gap - step * (4.0 * old_accel[3:6] + 2.0 * force[3:6])
    second = 12.0 * gap + 6.0 * step * (old_accel[3:6] + force[3:6])
    pos = targets[0:3] + step * step * (first / 24.0 + second / 120.0)
    vel = targets[3:6] + step * (first / 6.0 + second / 24.0)
    return jnp.concatenate([pos, vel, force], axis=0)

FOUR = 4
ORDER = sorted(
    ((a, b) for a in range(RING) for b in range(RING)), key=lambda p: ((p[0] + 1) // 2 + (p[1] + 1) // 2, p)
)
EARLY = 5


def kernel(
    gravity, soften,
    pos_in, vel_in, mass_in, old_in, index_in, level_in, tile_in, offset_in,
    state_ref, image_ref,
    pos_ref, vel_ref, mass_ref, old_ref, index_ref, level_ref, tile_ref, offset_ref,
    source, small, own, own_in, rest, rest_in, settled, targets, source_f, moments, near_f, dots_f,
    part, part_in, spread, gathered, tiles, tiles_in, tiles_all, left, right,
    load_sem, send_sem, recv_sem, deposit_sem,
):
    team, loop = lax.axis_index("team"), lax.axis_index("loop")
    zh, y, c = team // 16, (team // 2) % 8, team % 2
    zl, x = loop // 4, loop % 4
    z = zh * 2 + zl

    def at(y, z, x, c):
        return ((z // 2) * 16 + y * 2 + c, (z % 2) * 4 + x)

    def step_of(s):
        away = (s + 1) // 2
        return away + (s + 1) % 2 * (8 - 2 * away)

    def y_peer(s, sign=1):
        return at((y + 8 + sign * step_of(s)) % 8, z, x, c)

    def z_peer(s):
        return at(y, (z + step_of(s)) % 8, x, c)

    def x_peer(s):
        return at(y, z, (x + s // 2) % 4, (c + s % 2) % 2)

    slots = range(1, RING)
    barrier = pltpu.get_barrier_semaphore()
    for s in reversed(slots):
        for peer in (y_peer(s), z_peer(s), x_peer(s)):
            pl.semaphore_signal(barrier, inc=1, device_id=peer, device_id_type=MESH)
    loads = [
        pltpu.make_async_copy(src, dst, load_sem.at[i])
        for i, (src, dst) in enumerate(
            (
                (pos_in, pos_ref), (vel_in, vel_ref), (mass_in, mass_ref), (index_in, index_ref),
                (old_in, old_ref), (level_in, level_ref), (tile_in, tile_ref), (offset_in, offset_ref),
            )
        )
    ]
    for one in loads:
        one.start()
    for one in loads:
        one.wait()

    def copy(stage, slot, src, dst, peer):
        return pltpu.make_async_remote_copy(
            src_ref=src,
            dst_ref=dst,
            send_sem=send_sem.at[stage],
            recv_sem=recv_sem.at[stage, slot],
            device_id=peer,
            device_id_type=MESH,
        )

    def await_all(stage, ref):
        copy(stage, 0, ref, ref, y_peer(1)).wait_recv()

    def await_sent(stage, ref):
        copy(stage, 0, ref, ref, y_peer(1)).wait_send()

    source[0, 0:3, :] = pos_ref[...]
    source[0, 3:6, :] = vel_ref[...]
    source[0, 6:7, :] = mass_ref[...].reshape(1, SRC)
    source[0, 7:8, :] = jnp.zeros((1, SRC), F32)
    small[...] = jnp.zeros_like(small)
    small[0:6, 0:ACT] = old_ref[...]
    small[6:7, 0:ACT] = level_ref[...].reshape(1, ACT).astype(F32)
    small[7:8, 0:ACT] = tile_ref[...].reshape(1, ACT).astype(F32)
    small[8:10, 0:ACT] = offset_ref[...].astype(F32)
    small[10:11, 0:ACT] = index_ref[...].reshape(1, ACT).astype(F32)
    place = x * 2 + c
    placed = pltpu.roll(small[...], place * ACT, 1)
    star = lax.broadcasted_iota(jnp.int32, (SRC, LANES), 0).astype(F32)
    lane = lax.broadcasted_iota(jnp.int32, (SRC, LANES), 1)
    chosen = jnp.where((star == placed[10:11]) & (lane // ACT == place), 1.0, 0.0).astype(BF16)
    pieces = jnp.concatenate(wide3(source[0]), axis=0).astype(BF16)
    picked = jnp.dot(pieces, chosen, preferred_element_type=F32)
    own[...] = picked[0:8] + picked[8:16] + picked[16:24]
    rest[...] = placed

    pl.semaphore_wait(barrier, 3 * (RING - 1))

    for s in reversed(slots):
        copy(2, s, source.at[0], source.at[s], z_peer(s)).start()
    for s in (4, 5, 2, 3, 6, 7, 1):
        copy(0, 0, own, own_in.at[s - 1], x_peer(s)).start()
    for s in slots:
        copy(1, 0, rest, rest_in.at[s - 1], x_peer(s)).start()

    def prepare_source(s):
        v = source[s]
        rows = slice(s * SRC, (s + 1) * SRC)
        source_f[rows, :] = jnp.transpose(features(v[0:3], v[3:6], None)[1]).astype(BF16)
        mass = v[6:7]
        sums = jnp.concatenate([v[0:3] * mass, v[3:6] * mass, mass, jnp.zeros_like(mass)], axis=0)
        moments[:, rows] = pad_rows(jnp.concatenate(wide3(sums), axis=0), 32).astype(BF16)

    def await_source(s):
        copy(2, s, source.at[0], source.at[s], z_peer(s)).wait_recv()

    def prepare_targets(first, last):
        t = jnp.concatenate([targets[s] for s in range(first, last)], axis=1)
        cut, f = features(t[0:3], t[3:6], soften)
        row = lax.broadcasted_iota(jnp.int32, f.shape, 0)
        lanes = slice(first * LANES, last * LANES)
        near_f[:, lanes] = jnp.where(row < cut, f, 0.0).astype(BF16)
        dots_f[:, lanes] = jnp.where(row < cut, 0.0, f).astype(BF16)

    def force_sums(s, first, last):
        lanes = pl.ds(pl.multiple_of(s * LANES, LANES), LANES)
        rows = slice(first * SRC, last * SRC)
        dist_sq = jnp.dot(source_f[rows, :], near_f[:, lanes], preferred_element_type=F32)
        dots = jnp.dot(source_f[rows, :], dots_f[:, lanes], preferred_element_type=F32)
        inverse = lax.rsqrt(dist_sq)
        inverse_sq = inverse * inverse
        strength = inverse * inverse_sq
        radial = (strength * inverse_sq) * dots
        plain = jnp.dot(moments[:, rows], strength.astype(BF16), preferred_element_type=F32)
        tilted = jnp.dot(moments[:, rows], radial.astype(BF16), preferred_element_type=F32)
        return plain[0:8] + plain[8:16] + plain[16:24], tilted[0:8] + tilted[8:16] + tilted[16:24]

    def combine(s, plain, tilted):
        t = targets[s]
        accel = plain[0:3] - t[0:3] * plain[6:7]
        jerk = (plain[3:6] - t[3:6] * plain[6:7]) - 3.0 * (tilted[0:3] - t[0:3] * tilted[6:7])
        part[s] = pad_rows(gravity * jnp.concatenate([accel, jerk], axis=0), 8)

    prepare_source(0)

    await_all(0, own_in)
    block = own[...]
    for s in slots:
        block = block + own_in[s - 1]
    targets[0] = block
    for s in reversed(slots):
        copy(3, s, targets.at[0], targets.at[s], y_peer(s)).start()
    prepare_targets(0, 1)
    for s in range(1, EARLY):
        await_source(s)
        prepare_source(s)
    plain, tilted = force_sums(0, 0, EARLY)

    await_all(1, rest_in)
    others = rest[...]
    for s in slots:
        others = others + rest_in[s - 1]
    settled[...] = others
    tiles[0] = others[7:8]
    for s in slots:
        copy(11, 0, tiles.at[0], tiles.at[s], z_peer(s)).start()
    image_ref[...] = jnp.zeros_like(image_ref)

    def await_targets(s):
        copy(3, s, targets.at[0], targets.at[s], y_peer(s)).wait_recv()

    await_targets(1)
    prepare_targets(1, 2)
    next_plain, next_tilted = force_sums(1, 0, EARLY)
    for s in range(EARLY, RING):
        await_source(s)
        prepare_source(s)
    more = force_sums(0, EARLY, RING)
    combine(0, plain + more[0], tilted + more[1])

    def give(s, first):
        back = (y + 8 - step_of(s)) % 8
        for q in (4, 5, 2, 3, 6, 7, 1, 0):
            if q >= first:
                peer = at(back, z, (x + q // 2) % 4, (c + q % 2) % 2)
                copy(4, 0, part.at[s], part_in.at[s * RING + q], peer).start()

    def slot_of(i):
        return jnp.where(i < 2, 2 * i + 1, jnp.where(i == 2, 7, jnp.where(i == 3, 5, 14 - 2 * i)))

    def force_step(i, carry):
        @pl.when(i == 1)
        def _():
            await_targets(3)
            prepare_targets(3, 4)

        @pl.when(i == 2)
        def _():
            for s in (2, 4, 5, 6, 7):
                await_targets(s)
            prepare_targets(4, RING)
            prepare_targets(2, 3)

        @pl.when(i == 3)
        def _():
            await_all(11, tiles.at[pl.ds(1, RING - 1)])
            for s in slots:
                copy(12, 0, tiles, tiles_in.at[s - 1], y_peer(s)).start()

        s = slot_of(i)
        give(slot_of(i - 1), 0)
        combine(s, *force_sums(s, 0, RING))
        return carry

    give(0, 1)
    more = force_sums(1, EARLY, RING)
    combine(1, next_plain + more[0], next_tilted + more[1])
    lax.fori_loop(1, RING - 1, force_step, 0)
    give(2, 0)

    await_sent(0, own_in)
    await_sent(1, rest_in)
    await_sent(2, source.at[pl.ds(1, RING - 1)])
    await_sent(3, targets.at[pl.ds(1, RING - 1)])
    await_sent(11, tiles.at[pl.ds(1, RING - 1)])
    await_sent(12, tiles_in)
    await_all(12, tiles_in)
    for i, (away_y, away_z) in enumerate(ORDER):
        tiles_all[i] = tiles_in[away_y - 1, away_z] if away_y else tiles[away_z]
    await_all(4, part_in.at[pl.ds(1, RING * RING - 1)])
    total = part[0] + jnp.sum(part_in[1:], axis=0)

    stars = targets[0]
    others = settled[...]
    state = correct(stars[0:6], total[0:6], others[0:6], others[6:7])
    centre_y = others[8:9] + (TILE_W / 16.0) * jnp.tanh(state[1:2])
    centre_x = others[9:10] + (TILE_W / 16.0) * jnp.tanh(state[0:1])
    mass = stars[6:7]
    spread[...] = jnp.concatenate([mass, mass * state[5:6] * state[5:6], centre_y, centre_x], axis=0)
    gathered[0] = spread[...]

    def deposit(i):
        away_y, away_z = ORDER[i]
        return pltpu.make_async_remote_copy(
            src_ref=spread,
            dst_ref=gathered.at[i],
            send_sem=send_sem.at[6],
            recv_sem=deposit_sem.at[i // FOUR],
            device_id=at((y + step_of(away_y)) % 8, (z + step_of(away_z)) % 8, x, c),
            device_id_type=MESH,
        )

    for i in range(1, len(ORDER)):
        deposit(i).start()

    def await_deposits(first, count):
        these = gathered.at[pl.ds(first, count)]
        pltpu.make_async_remote_copy(
            src_ref=these,
            dst_ref=these,
            send_sem=send_sem.at[6],
            recv_sem=deposit_sem.at[first // FOUR],
            device_id=y_peer(1),
            device_id_type=MESH,
        ).wait_recv()

    mine = (team * 8 + loop).astype(F32)
    reach = (40.0 / TILE_W) * math.sqrt(0.5 * math.log2(math.e))
    cell = (lax.broadcasted_iota(jnp.int32, (TILE_W, LANES), 0).astype(F32) + 0.5) * reach

    def kernel_of(centre):
        scaled = cell - centre * reach
        return jnp.exp2(-(scaled * scaled))

    def build(half, blocks):
        for b, (rows, tile) in enumerate(blocks):
            here = tile == mine
            rows_y, rows_x = kernel_of(rows[2:3]), kernel_of(rows[3:4])
            lanes = slice((half * FOUR + b) * LANES, (half * FOUR + b + 1) * LANES)
            left[0:TILE_W, lanes] = (jnp.where(here, rows[0:1], 0.0) * rows_y).astype(BF16)
            left[TILE_W:, lanes] = (jnp.where(here, rows[1:2], 0.0) * rows_y).astype(BF16)
            right[:, lanes] = rows_x.astype(BF16)

    def add_stars():
        out = lax.dot_general(
            left[...], right[...], (((1,), (1,)), ((), ())), preferred_element_type=F32
        )
        image_ref[...] += out.reshape(2, 1, TILE_W, TILE_W)

    shifted = pltpu.roll(pad_rows(state, 16), (LANES - place * ACT) % LANES, 1)
    state_ref[...] = shifted[0:12, 0:ACT]

    def build_four(half, first):
        build(half, [(gathered[first + k], tiles_all[first + k]) for k in range(FOUR)])

    await_deposits(1, FOUR - 1)
    build_four(0, 0)
    await_deposits(FOUR, FOUR)
    build_four(1, FOUR)
    add_stars()

    def deposit_step(j, carry):
        for half in (0, 1):
            first = (2 * j + half) * FOUR
            await_deposits(first, FOUR)
            build_four(half, first)
        add_stars()
        return carry

    lax.fori_loop(1, RING, deposit_step, 0)
    await_sent(4, part_in.at[pl.ds(1, RING * RING - 1)])
    await_sent(6, gathered.at[pl.ds(1, len(ORDER) - 1)])


def shards(*arrays):
    stars = SRC * RING**3
    stage_count = 13
    vmem = pl.BlockSpec(memory_space=pltpu.VMEM)
    outputs = (
        jax.ShapeDtypeStruct((12, ACT), F32),
        jax.ShapeDtypeStruct((2, 1, TILE_W, TILE_W), F32),
    )
    return pl.pallas_call(
        functools.partial(kernel, 1.0 / stars, float(stars) ** (-2.0 / 3.0)),
        out_shape=outputs,
        in_specs=[pl.BlockSpec(memory_space=pl.ANY)] * len(arrays),
        out_specs=(vmem, vmem),
        scratch_shapes=[pltpu.VMEM(v.shape, v.dtype) for v in arrays] + [
            pltpu.VMEM((RING, 8, SRC), F32),
            pltpu.VMEM((16, LANES), F32),
            pltpu.VMEM((8, LANES), F32),
            pltpu.VMEM((RING - 1, 8, LANES), F32),
            pltpu.VMEM((16, LANES), F32),
            pltpu.VMEM((RING - 1, 16, LANES), F32),
            pltpu.VMEM((16, LANES), F32),
            pltpu.VMEM((RING, 8, LANES), F32),
            pltpu.VMEM((RING * SRC, LANES), BF16),
            pltpu.VMEM((32, RING * SRC), BF16),
            pltpu.VMEM((LANES, RING * LANES), BF16),
            pltpu.VMEM((LANES, RING * LANES), BF16),
            pltpu.VMEM((RING, 8, LANES), F32),
            pltpu.VMEM((RING * RING, 8, LANES), F32),
            pltpu.VMEM((4, LANES), F32),
            pltpu.VMEM((RING * RING, 4, LANES), F32),
            pltpu.VMEM((RING, 1, LANES), F32),
            pltpu.VMEM((RING - 1, RING, 1, LANES), F32),
            pltpu.VMEM((RING * RING, 1, LANES), F32),
            pltpu.VMEM((2 * TILE_W, 2 * FOUR * LANES), BF16),
            pltpu.VMEM((TILE_W, 2 * FOUR * LANES), BF16),
            pltpu.SemaphoreType.DMA((len(arrays),)),
            pltpu.SemaphoreType.DMA((stage_count,)),
            pltpu.SemaphoreType.DMA((stage_count, RING)),
            pltpu.SemaphoreType.DMA((RING * RING // FOUR,)),
        ],
        compiler_params=pltpu.CompilerParams(
            collective_id=0, has_side_effects=True, vmem_limit_bytes=48 << 20
        ),
        name="cluster_step",
    )(*[pltpu.with_memory_space_constraint(v, pltpu.HBM) for v in arrays])


def solution(mesh):
    both = ("team", "loop")
    columns, rows = P(None, both), P(both)
    return jax.shard_map(
        shards,
        mesh=mesh,
        in_specs=(columns, columns, rows, columns, rows, rows, rows, columns),
        out_specs=(columns, P(None, both, None, None)),
        check_vma=False,
    )
```

```python
import functools
import math

import jax
import jax.numpy as jnp
from jax import lax
from jax.experimental import pallas as pl
from jax.experimental.pallas import tpu as pltpu
from jax.sharding import PartitionSpec as P

MESH = pl.DeviceIdType.MESH
F32, BF16 = jnp.float32, jnp.bfloat16
RING = 8
SRC = 512
ACT = 16
LANES = 128
TILE_W = 128


def split3(v):
    a = v.astype(BF16)
    r = v - a.astype(F32)
    b = r.astype(BF16)
    return a, b, (r - b.astype(F32)).astype(BF16)


def wide3(v):
    return [p.astype(F32) for p in split3(v)]


def wide2(v):
    a = v.astype(BF16).astype(F32)
    return a, (v - a).astype(BF16).astype(F32)


def coarse(v):
    return jnp.round(v * 32.0) * (1.0 / 32.0)


def pad_rows(v, rows):
    gap = jnp.zeros((rows - v.shape[0], v.shape[1]), v.dtype)
    return jnp.concatenate([v, gap], axis=0)


def features(pos, vel, soften):
    h, u = coarse(pos), coarse(vel)
    l, m = pos - h, vel - u
    l1, l2 = wide2(l)
    m1, m2 = wide2(m)
    total = lambda v: jnp.sum(v, axis=0, keepdims=True)
    hh = wide3(total(h * h))
    hl = wide3(total(2.0 * h * l + l * l) + (0.0 if soften is None else soften))
    hu = wide3(total(h * u))
    hm = wide3(total(h * m + l * u + l * m))
    ones = [jnp.ones_like(h)]
    if soften is None:
        near = [h] + hh + ones + [h, h, l1, l2, l1, l1, l2] + hl + ones
        dots = [h, u] + hu + ones + [h, h, m1, m2, l1, l2, u, u, l1, l1, l2, m1, m1, m2] + hm + ones
    else:
        near = [-2.0 * h] + ones + hh
        near += [-2.0 * l1, -2.0 * l2, -2.0 * h, -2.0 * h, -2.0 * l1, -2.0 * l2, -2.0 * l1] + ones + hl
        dots = [-u, -h] + ones + hu
        dots += [-m1, -m2, -h, -h, -u, -u, -l1, -l2, -m1, -m2, -m1, -l1, -l2, -l1] + ones + hm
    near = jnp.concatenate(near, axis=0)
    return near.shape[0], pad_rows(jnp.concatenate([near] + dots, axis=0), LANES)


def correct(targets, force, old_accel, level):
    step = jnp.exp2(-level)
    gap = old_accel[0:3] - force[0:3]
    first = -6.0 * gap - step * (4.0 * old_accel[3:6] + 2.0 * force[3:6])
    second = 12.0 * gap + 6.0 * step * (old_accel[3:6] + force[3:6])
    pos = targets[0:3] + step * step * (first / 24.0 + second / 120.0)
    vel = targets[3:6] + step * (first / 6.0 + second / 24.0)
    return jnp.concatenate([pos, vel, force], axis=0)

FOUR = 4
ORDER = sorted(
    ((a, b) for a in range(RING) for b in range(RING)), key=lambda p: ((p[0] + 1) // 2 + (p[1] + 1) // 2, p)
)
EARLY = 5


def kernel(
    gravity, soften,
    pos_in, vel_in, mass_in, old_in, index_in, level_in, tile_in, offset_in,
    state_ref, image_ref,
    pos_ref, vel_ref, mass_ref, old_ref, index_ref, level_ref, tile_ref, offset_ref,
    source, small, own, own_in, rest, rest_in, settled, targets, source_f, moments, near_f, dots_f,
    part, part_in, spread, gathered, tiles, tiles_in, tiles_all, left, right,
    load_sem, send_sem, recv_sem, deposit_sem,
):
    team, loop = lax.axis_index("team"), lax.axis_index("loop")
    zh, y, c = team // 16, (team // 2) % 8, team % 2
    zl, x = loop // 4, loop % 4
    z = zh * 2 + zl

    def at(y, z, x, c):
        return ((z // 2) * 16 + y * 2 + c, (z % 2) * 4 + x)

    def step_of(s):
        away = (s + 1) // 2
        return away + (s + 1) % 2 * (8 - 2 * away)

    def y_peer(s, sign=1):
        return at((y + 8 + sign * step_of(s)) % 8, z, x, c)

    def z_peer(s):
        return at(y, (z + step_of(s)) % 8, x, c)

    def x_peer(s):
        return at(y, z, (x + s // 2) % 4, (c + s % 2) % 2)

    slots = range(1, RING)
    barrier = pltpu.get_barrier_semaphore()
    for s in reversed(slots):
        for peer in (y_peer(s), z_peer(s), x_peer(s)):
            pl.semaphore_signal(barrier, inc=1, device_id=peer, device_id_type=MESH)
    loads = [
        pltpu.make_async_copy(src, dst, load_sem.at[i])
        for i, (src, dst) in enumerate(
            (
                (pos_in, pos_ref), (vel_in, vel_ref), (mass_in, mass_ref), (index_in, index_ref),
                (old_in, old_ref), (level_in, level_ref), (tile_in, tile_ref), (offset_in, offset_ref),
            )
        )
    ]
    for one in loads:
        one.start()
    for one in loads:
        one.wait()

    def copy(stage, slot, src, dst, peer):
        return pltpu.make_async_remote_copy(
            src_ref=src,
            dst_ref=dst,
            send_sem=send_sem.at[stage],
            recv_sem=recv_sem.at[stage, slot],
            device_id=peer,
            device_id_type=MESH,
        )

    def await_all(stage, ref):
        copy(stage, 0, ref, ref, y_peer(1)).wait_recv()

    def await_sent(stage, ref):
        copy(stage, 0, ref, ref, y_peer(1)).wait_send()

    source[0, 0:3, :] = pos_ref[...]
    source[0, 3:6, :] = vel_ref[...]
    source[0, 6:7, :] = mass_ref[...].reshape(1, SRC)
    source[0, 7:8, :] = jnp.zeros((1, SRC), F32)
    small[...] = jnp.zeros_like(small)
    small[0:6, 0:ACT] = old_ref[...]
    small[6:7, 0:ACT] = level_ref[...].reshape(1, ACT).astype(F32)
    small[7:8, 0:ACT] = tile_ref[...].reshape(1, ACT).astype(F32)
    small[8:10, 0:ACT] = offset_ref[...].astype(F32)
    small[10:11, 0:ACT] = index_ref[...].reshape(1, ACT).astype(F32)
    place = x * 2 + c
    placed = pltpu.roll(small[...], place * ACT, 1)
    star = lax.broadcasted_iota(jnp.int32, (SRC, LANES), 0).astype(F32)
    lane = lax.broadcasted_iota(jnp.int32, (SRC, LANES), 1)
    chosen = jnp.where((star == placed[10:11]) & (lane // ACT == place), 1.0, 0.0).astype(BF16)
    pieces = jnp.concatenate(wide3(source[0]), axis=0).astype(BF16)
    picked = jnp.dot(pieces, chosen, preferred_element_type=F32)
    own[...] = picked[0:8] + picked[8:16] + picked[16:24]
    rest[...] = placed

    pl.semaphore_wait(barrier, 3 * (RING - 1))

    for s in reversed(slots):
        copy(2, s, source.at[0], source.at[s], z_peer(s)).start()
    for s in (4, 5, 2, 3, 6, 7, 1):
        copy(0, 0, own, own_in.at[s - 1], x_peer(s)).start()
    for s in slots:
        copy(1, 0, rest, rest_in.at[s - 1], x_peer(s)).start()

    def prepare_source(s):
        v = source[s]
        rows = slice(s * SRC, (s + 1) * SRC)
        source_f[rows, :] = jnp.transpose(features(v[0:3], v[3:6], None)[1]).astype(BF16)
        mass = v[6:7]
        sums = jnp.concatenate([v[0:3] * mass, v[3:6] * mass, mass, jnp.zeros_like(mass)], axis=0)
        moments[:, rows] = pad_rows(jnp.concatenate(wide3(sums), axis=0), 32).astype(BF16)

    def await_source(s):
        copy(2, s, source.at[0], source.at[s], z_peer(s)).wait_recv()

    def prepare_targets(first, last):
        t = jnp.concatenate([targets[s] for s in range(first, last)], axis=1)
        cut, f = features(t[0:3], t[3:6], soften)
        row = lax.broadcasted_iota(jnp.int32, f.shape, 0)
        lanes = slice(first * LANES, last * LANES)
        near_f[:, lanes] = jnp.where(row < cut, f, 0.0).astype(BF16)
        dots_f[:, lanes] = jnp.where(row < cut, 0.0, f).astype(BF16)

    def force_sums(s, first, last):
        lanes = pl.ds(pl.multiple_of(s * LANES, LANES), LANES)
        rows = slice(first * SRC, last * SRC)
        dist_sq = jnp.dot(source_f[rows, :], near_f[:, lanes], preferred_element_type=F32)
        dots = jnp.dot(source_f[rows, :], dots_f[:, lanes], preferred_element_type=F32)
        inverse = lax.rsqrt(dist_sq)
        inverse_sq = inverse * inverse
        strength = inverse * inverse_sq
        radial = (strength * inverse_sq) * dots
        plain = jnp.dot(moments[:, rows], strength.astype(BF16), preferred_element_type=F32)
        tilted = jnp.dot(moments[:, rows], radial.astype(BF16), preferred_element_type=F32)
        return plain[0:8] + plain[8:16] + plain[16:24], tilted[0:8] + tilted[8:16] + tilted[16:24]

    def combine(s, plain, tilted):
        t = targets[s]
        accel = plain[0:3] - t[0:3] * plain[6:7]
        jerk = (plain[3:6] - t[3:6] * plain[6:7]) - 3.0 * (tilted[0:3] - t[0:3] * tilted[6:7])
        part[s] = pad_rows(gravity * jnp.concatenate([accel, jerk], axis=0), 8)

    prepare_source(0)

    await_all(0, own_in)
    block = own[...]
    for s in slots:
        block = block + own_in[s - 1]
    targets[0] = block
    for s in reversed(slots):
        copy(3, s, targets.at[0], targets.at[s], y_peer(s)).start()
    prepare_targets(0, 1)
    for s in range(1, EARLY):
        await_source(s)
        prepare_source(s)
    plain, tilted = force_sums(0, 0, EARLY)

    await_all(1, rest_in)
    others = rest[...]
    for s in slots:
        others = others + rest_in[s - 1]
    settled[...] = others
    tiles[0] = others[7:8]
    for s in slots:
        copy(11, 0, tiles.at[0], tiles.at[s], z_peer(s)).start()
    image_ref[...] = jnp.zeros_like(image_ref)

    def await_targets(s):
        copy(3, s, targets.at[0], targets.at[s], y_peer(s)).wait_recv()

    await_targets(1)
    prepare_targets(1, 2)
    next_plain, next_tilted = force_sums(1, 0, EARLY)
    for s in range(EARLY, RING):
        await_source(s)
        prepare_source(s)

    def give(s, first):
        back = (y + 8 - step_of(s)) % 8
        for q in (4, 5, 2, 3, 6, 7, 1, 0):
            if q >= first:
                peer = at(back, z, (x + q // 2) % 4, (c + q % 2) % 2)
                copy(4, 0, part.at[s], part_in.at[s * RING + q], peer).start()

    def slot_of(i):
        return jnp.where(i < 2, 2 * i + 1, jnp.where(i == 2, 7, jnp.where(i == 3, 5, 14 - 2 * i)))

    def force_step(i, carry):
        @pl.when(i == 1)
        def _():
            await_targets(3)
            prepare_targets(3, 4)

        @pl.when(i == 2)
        def _():
            for s in (2, 4, 5, 6, 7):
                await_targets(s)
            prepare_targets(4, RING)
            prepare_targets(2, 3)

        @pl.when(i == 3)
        def _():
            await_all(11, tiles.at[pl.ds(1, RING - 1)])
            for s in slots:
                copy(12, 0, tiles, tiles_in.at[s - 1], y_peer(s)).start()

        s = slot_of(i)
        give(slot_of(i - 1), 0)
        combine(s, *force_sums(s, 0, RING))
        return carry

    more = force_sums(1, EARLY, RING)
    combine(1, next_plain + more[0], next_tilted + more[1])
    lax.fori_loop(1, RING - 1, force_step, 0)
    give(2, 0)
    more = force_sums(0, EARLY, RING)
    combine(0, plain + more[0], tilted + more[1])
    give(0, 1)

    await_sent(0, own_in)
    await_sent(1, rest_in)
    await_sent(2, source.at[pl.ds(1, RING - 1)])
    await_sent(3, targets.at[pl.ds(1, RING - 1)])
    await_sent(11, tiles.at[pl.ds(1, RING - 1)])
    await_sent(12, tiles_in)
    await_all(12, tiles_in)
    for i, (away_y, away_z) in enumerate(ORDER):
        tiles_all[i] = tiles_in[away_y - 1, away_z] if away_y else tiles[away_z]
    await_all(4, part_in.at[pl.ds(1, RING * RING - 1)])
    total = part[0] + jnp.sum(part_in[1:], axis=0)

    stars = targets[0]
    others = settled[...]
    state = correct(stars[0:6], total[0:6], others[0:6], others[6:7])
    centre_y = others[8:9] + (TILE_W / 16.0) * jnp.tanh(state[1:2])
    centre_x = others[9:10] + (TILE_W / 16.0) * jnp.tanh(state[0:1])
    mass = stars[6:7]
    spread[...] = jnp.concatenate([mass, mass * state[5:6] * state[5:6], centre_y, centre_x], axis=0)
    gathered[0] = spread[...]

    def deposit(i):
        away_y, away_z = ORDER[i]
        return pltpu.make_async_remote_copy(
            src_ref=spread,
            dst_ref=gathered.at[i],
            send_sem=send_sem.at[6],
            recv_sem=deposit_sem.at[i // FOUR],
            device_id=at((y + step_of(away_y)) % 8, (z + step_of(away_z)) % 8, x, c),
            device_id_type=MESH,
        )

    for i in range(1, len(ORDER)):
        deposit(i).start()

    def await_deposits(first, count):
        these = gathered.at[pl.ds(first, count)]
        pltpu.make_async_remote_copy(
            src_ref=these,
            dst_ref=these,
            send_sem=send_sem.at[6],
            recv_sem=deposit_sem.at[first // FOUR],
            device_id=y_peer(1),
            device_id_type=MESH,
        ).wait_recv()

    mine = (team * 8 + loop).astype(F32)
    reach = (40.0 / TILE_W) * math.sqrt(0.5 * math.log2(math.e))
    cell = (lax.broadcasted_iota(jnp.int32, (TILE_W, LANES), 0).astype(F32) + 0.5) * reach

    def kernel_of(centre):
        scaled = cell - centre * reach
        return jnp.exp2(-(scaled * scaled))

    def build(half, blocks):
        for b, (rows, tile) in enumerate(blocks):
            here = tile == mine
            rows_y, rows_x = kernel_of(rows[2:3]), kernel_of(rows[3:4])
            lanes = slice((half * FOUR + b) * LANES, (half * FOUR + b + 1) * LANES)
            left[0:TILE_W, lanes] = (jnp.where(here, rows[0:1], 0.0) * rows_y).astype(BF16)
            left[TILE_W:, lanes] = (jnp.where(here, rows[1:2], 0.0) * rows_y).astype(BF16)
            right[:, lanes] = rows_x.astype(BF16)

    def add_stars():
        out = lax.dot_general(
            left[...], right[...], (((1,), (1,)), ((), ())), preferred_element_type=F32
        )
        image_ref[...] += out.reshape(2, 1, TILE_W, TILE_W)

    shifted = pltpu.roll(pad_rows(state, 16), (LANES - place * ACT) % LANES, 1)
    state_ref[...] = shifted[0:12, 0:ACT]

    def build_four(half, first):
        build(half, [(gathered[first + k], tiles_all[first + k]) for k in range(FOUR)])

    await_deposits(1, FOUR - 1)
    build_four(0, 0)
    await_deposits(FOUR, FOUR)
    build_four(1, FOUR)
    add_stars()

    def deposit_step(j, carry):
        for half in (0, 1):
            first = (2 * j + half) * FOUR
            await_deposits(first, FOUR)
            build_four(half, first)
        add_stars()
        return carry

    lax.fori_loop(1, RING, deposit_step, 0)
    await_sent(4, part_in.at[pl.ds(1, RING * RING - 1)])
    await_sent(6, gathered.at[pl.ds(1, len(ORDER) - 1)])


def shards(*arrays):
    stars = SRC * RING**3
    stage_count = 13
    vmem = pl.BlockSpec(memory_space=pltpu.VMEM)
    outputs = (
        jax.ShapeDtypeStruct((12, ACT), F32),
        jax.ShapeDtypeStruct((2, 1, TILE_W, TILE_W), F32),
    )
    return pl.pallas_call(
        functools.partial(kernel, 1.0 / stars, float(stars) ** (-2.0 / 3.0)),
        out_shape=outputs,
        in_specs=[pl.BlockSpec(memory_space=pl.ANY)] * len(arrays),
        out_specs=(vmem, vmem),
        scratch_shapes=[pltpu.VMEM(v.shape, v.dtype) for v in arrays] + [
            pltpu.VMEM((RING, 8, SRC), F32),
            pltpu.VMEM((16, LANES), F32),
            pltpu.VMEM((8, LANES), F32),
            pltpu.VMEM((RING - 1, 8, LANES), F32),
            pltpu.VMEM((16, LANES), F32),
            pltpu.VMEM((RING - 1, 16, LANES), F32),
            pltpu.VMEM((16, LANES), F32),
            pltpu.VMEM((RING, 8, LANES), F32),
            pltpu.VMEM((RING * SRC, LANES), BF16),
            pltpu.VMEM((32, RING * SRC), BF16),
            pltpu.VMEM((LANES, RING * LANES), BF16),
            pltpu.VMEM((LANES, RING * LANES), BF16),
            pltpu.VMEM((RING, 8, LANES), F32),
            pltpu.VMEM((RING * RING, 8, LANES), F32),
            pltpu.VMEM((4, LANES), F32),
            pltpu.VMEM((RING * RING, 4, LANES), F32),
            pltpu.VMEM((RING, 1, LANES), F32),
            pltpu.VMEM((RING - 1, RING, 1, LANES), F32),
            pltpu.VMEM((RING * RING, 1, LANES), F32),
            pltpu.VMEM((2 * TILE_W, 2 * FOUR * LANES), BF16),
            pltpu.VMEM((TILE_W, 2 * FOUR * LANES), BF16),
            pltpu.SemaphoreType.DMA((len(arrays),)),
            pltpu.SemaphoreType.DMA((stage_count,)),
            pltpu.SemaphoreType.DMA((stage_count, RING)),
            pltpu.SemaphoreType.DMA((RING * RING // FOUR,)),
        ],
        compiler_params=pltpu.CompilerParams(
            collective_id=0, has_side_effects=True, vmem_limit_bytes=48 << 20
        ),
        name="cluster_step",
    )(*[pltpu.with_memory_space_constraint(v, pltpu.HBM) for v in arrays])


def solution(mesh):
    both = ("team", "loop")
    columns, rows = P(None, both), P(both)
    return jax.shard_map(
        shards,
        mesh=mesh,
        in_specs=(columns, columns, rows, columns, rows, rows, rows, columns),
        out_specs=(columns, P(None, both, None, None)),
        check_vma=False,
    )
```
